32 devices in a mesh: dp: 2 (over y), pipe: 4 (over z), expert: 4 (over x, core).
Axes of the slice: x: 2, y: 2, z: 4, core: 2. Of those that a mesh axis runs over, the one named last changes fastest.
Arguments:
- fresh: bfloat16 [512, 6144], P(('dp', 'expert')), may hold values from -6 to 6
- cotangent: bfloat16 [512, 6144], P(('dp', 'expert')), may hold values from -6 to 6
- prev_out: bfloat16 [4, 512, 6144], P('pipe', ('dp', 'expert')), may hold values from -6 to 6
- prev_grad: bfloat16 [4, 512, 6144], P('pipe', ('dp', 'expert')), may hold values from -6 to 6
- saved_in: bfloat16 [4, 512, 6144], P('pipe', ('dp', 'expert')), may hold values from -6 to 6
- route_fwd: int32 [4, 512, 2], P('pipe', ('dp', 'expert')), may hold values from 0 to 3, all different within a row; in each aligned block of 64 rows (0 to 63, 64 to 127, ..., all dimensions but the last counted through in order) at most 64 rows name the same one
- route_bwd: int32 [4, 512, 2], P('pipe', ('dp', 'expert')), may hold values from 0 to 3, all different within a row; in each aligned block of 64 rows (0 to 63, 64 to 127, ..., all dimensions but the last counted through in order) at most 64 rows name the same one
- router: bfloat16 [4, 6144, 4], P('pipe'), may hold values from -0.078125 to 0.078125
- gate_up: bfloat16 [4, 4, 6144, 256], P('pipe', 'expert'), may hold values from -0.078125 to 0.078125
- down: bfloat16 [4, 4, 128, 6144], P('pipe', 'expert'), may hold values from -0.5 to 0.5
Outputs:
- section_out: bfloat16 [4, 512, 6144], P('pipe', ('dp', 'expert'))
- input_grad: bfloat16 [4, 512, 6144], P('pipe', ('dp', 'expert'))
- grad_gate_up: bfloat16 [4, 4, 6144, 256], P('pipe', 'expert', 'dp')
- grad_down: bfloat16 [4, 4, 128, 6144], P('pipe', 'expert', None, 'dp')
- grad_router: float32 [4, 6144, 4], P('pipe', ('dp', 'expert'))
The draws below stay inside these ranges and needn't reach their ends.
Inputs may be any that keep to these rules, and one draw needn't show every extreme that they name: `route_fwd`: each row names two different experts; in the 64 rows of one device no expert is named by more than 64 rows, and some expert reaches 64. `route_bwd`: each row names two different experts; in the 64 rows of one device no expert is named by more than 64 rows, and some expert reaches 64.
All inputs are finite; a program needn't handle non-finite values.
Results may differ from the reference program's by a relative error of at most 0.015.
Values may be sent and summed in bfloat16 or wider, within the bound.
A program may use at most 128 MiB of HBM per device.

```python
import math
import jax
import jax.numpy as jnp
import numpy as np
from jax import lax

D = 6144
FF = 128
TOK = 64
SECTIONS = 4
EXPERTS = 4
TOKENS = 512
CAP = 64
CAP2 = 32
N_DP = 2
N_EXPERT = 4


def levels(own_key, dims, pieces, smallest, top_value):
    loudness = 1.0
    for axis_at, blocks in pieces:
        heights = jax.random.uniform(jax.random.fold_in(jax.random.fold_in(own_key, 6), axis_at), (blocks,), jnp.float32, smallest / len(pieces), top_value / len(pieces))
        loudness = loudness * jnp.repeat(jnp.exp(heights), dims[axis_at] // blocks).reshape((-1,) + (1,) * (len(dims) - 1 - axis_at))
    return loudness


def deal_out(stream_key, own, number, rows, count, top, reach, lean):
    sequence = jax.random.permutation(stream_key, count)
    crowded, usual = load_shares(count, rows * top, reach, lean, True), load_shares(count, rows * top, reach, lean, False)
    places = jnp.arange(count)

    def named(tallies, offset_by):
        used = int((tallies > 0).sum())
        fixed = max(1, used // 4)
        passed = fixed + (places - fixed + offset_by * (used - fixed)) % max(1, count - fixed)
        return jnp.zeros((count,), jnp.int32).at[sequence[jnp.where(places < fixed, places, passed)]].set(jnp.asarray(tallies, jnp.int32))

    tallies = jnp.where(number % 4 == 0, named(crowded, number // 4), named(usual, number - number // 4 - 1))
    mixed = jax.random.permutation(jax.random.fold_in(own, 3), count)
    donor, taker = mixed[0:count // 2 * 2:2], mixed[1:count // 2 * 2:2]
    slack = jnp.minimum(tallies[donor] - 1, reach - tallies[taker]) // 2
    slack = jnp.where((donor == sequence[0]) | (taker == sequence[0]) | (tallies[taker] == 0), 0, jnp.maximum(slack, 0))
    passed = jax.random.randint(jax.random.fold_in(own, 4), (count // 2,), 0, 1 << 20) % (slack + 1)
    tallies = tallies.at[donor].add(-passed).at[taker].add(passed)
    members = jnp.searchsorted(jnp.cumsum(tallies), jnp.arange(rows * top), side="right").astype(jnp.int32)
    listing = members.reshape(top, rows).T
    listing = listing[jax.random.permutation(jax.random.fold_in(own, 1), rows)]
    offset_by = jax.random.randint(jax.random.fold_in(own, 2), (rows, 1), 0, top)
    return jnp.take_along_axis(listing, (jnp.arange(top)[None, :] + offset_by) % top, axis=1)


def load_shares(amount, total, most, slope, full):
    loads = [(1 << 20) // math.isqrt(standing ** slope) + 1 for standing in range(1, amount + 1)]
    largest = most if full else min(most, max(-(-total // amount), total * loads[0] // sum(loads)))
    least = 1 if total - largest >= amount - 1 else 0
    counts, surplus = [largest] + [least] * (amount - 1), total - largest - least * (amount - 1)
    while surplus > 0:
        candidates = [i for i in range(1, amount) if counts[i] < largest] or [i for i in range(1, amount) if counts[i] < most]
        whole, budget = sum([loads[i] for i in candidates]), surplus
        for i in candidates:
            more = min(most - counts[i], max(1, budget * loads[i] // whole), surplus)
            counts[i] = counts[i] + more
            surplus = surplus - more
    return np.array(counts)


def noise(own_key, dims, scale, bound, pieces=(), kind=jnp.bfloat16):
    factor_of = levels(own_key, dims, pieces, -0.22, 0.18) if pieces else 1.0
    drawn = jax.random.normal(own_key, dims, jnp.float32) * scale * factor_of
    return jnp.minimum(jnp.maximum(drawn, -bound), bound).astype(kind)


def setup_inputs(seed: int = 0) -> dict:
    keys = jax.random.split(jax.random.key(seed), 11)
    fresh = noise(keys[0], (TOKENS, D), 1.0, 6.0, ((0, 8),))
    cotangent = noise(keys[1], (TOKENS, D), 1.0, 6.0, ((0, 8),))
    prev_out = noise(keys[2], (SECTIONS, TOKENS, D), 1.0, 6.0, ((0, 4), (1, 8)))
    prev_grad = noise(keys[3], (SECTIONS, TOKENS, D), 1.0, 6.0, ((0, 4), (1, 8)))
    saved_in = noise(keys[4], (SECTIONS, TOKENS, D), 1.0, 6.0, ((0, 4), (1, 8)))
    route_fwd_keys = jax.random.split(jax.random.fold_in(keys[5], 1), SECTIONS * TOKENS // TOK)
    route_fwd_turns = jax.random.permutation(jax.random.fold_in(keys[5], 3), SECTIONS * TOKENS // TOK)
    route_fwd = jax.vmap(lambda own, number: deal_out(jax.random.fold_in(keys[5], 2), own, number, TOK, EXPERTS, 2, CAP, 2))(route_fwd_keys, route_fwd_turns).reshape((SECTIONS, TOKENS, 2))
    route_bwd_keys = jax.random.split(jax.random.fold_in(keys[6], 1), SECTIONS * TOKENS // TOK)
    route_bwd_turns = jax.random.permutation(jax.random.fold_in(keys[6], 3), SECTIONS * TOKENS // TOK)
    route_bwd = jax.vmap(lambda own, number: deal_out(jax.random.fold_in(keys[6], 2), own, number, TOK, EXPERTS, 2, CAP, 2))(route_bwd_keys, route_bwd_turns).reshape((SECTIONS, TOKENS, 2))
    router = noise(keys[7], (SECTIONS, D, EXPERTS), D ** -0.5, 0.078125, ((0, 4),))
    gate_up = noise(keys[8], (SECTIONS, EXPERTS, D, 2 * FF), D ** -0.5, 0.078125, ((0, 4), (1, 4)))
    down = noise(keys[9], (SECTIONS, EXPERTS, FF, D), FF ** -0.5, 0.5, ((0, 4), (1, 4)))
    return dict(fresh=fresh, cotangent=cotangent, prev_out=prev_out, prev_grad=prev_grad, saved_in=saved_in, route_fwd=route_fwd, route_bwd=route_bwd, router=router, gate_up=gate_up, down=down)


EPSILON = 1e-05

def normalize(values_in):
    values = values_in.astype(jnp.float32)
    spread = jnp.sqrt(lax.optimization_barrier(jnp.mean(values * values, axis=-1, keepdims=True)) + EPSILON)
    return (values / spread, spread)

def gate_pair(normed, router_w, routes):
    logits = jnp.dot(normed, router_w, preferred_element_type=jnp.float32)
    onehot = (routes[:, :, None] == jnp.arange(EXPERTS, dtype=jnp.int32)[None, None, :]).astype(jnp.float32)
    chosen = lax.optimization_barrier(jnp.sum(onehot * logits[:, None, :], axis=2))
    first_gate = jax.nn.sigmoid(chosen[:, 0] - chosen[:, 1])
    second_gate = jax.nn.sigmoid(chosen[:, 1] - chosen[:, 0])
    return (first_gate, second_gate, onehot)

def expert_forward(inputs, gate_up_w, down_w):
    projected = jnp.dot(inputs, gate_up_w, preferred_element_type=jnp.float32)
    pre_gate = projected[:, :FF]
    pre_up = projected[:, FF:]
    hidden = (pre_gate * jax.nn.sigmoid(pre_gate) * pre_up).astype(jnp.bfloat16)
    return jnp.dot(hidden, down_w, preferred_element_type=jnp.float32).astype(jnp.bfloat16)

def expert_backward(inputs, upstream, weight, gate_up_w, down_w):
    projected = jnp.dot(inputs, gate_up_w, preferred_element_type=jnp.float32)
    pre_gate = projected[:, :FF]
    pre_up = projected[:, FF:]
    sigmoid_gate = jax.nn.sigmoid(pre_gate)
    active = pre_gate * sigmoid_gate
    hidden = (active * pre_up).astype(jnp.bfloat16)
    output = jnp.dot(hidden, down_w, preferred_element_type=jnp.float32).astype(jnp.bfloat16)
    gate_grad = lax.optimization_barrier(jnp.sum(upstream.astype(jnp.float32) * output.astype(jnp.float32), axis=1)).astype(jnp.bfloat16)
    out_grad = (weight.astype(jnp.float32)[:, None] * upstream.astype(jnp.float32)).astype(jnp.bfloat16)
    hidden_grad = jnp.dot(out_grad, down_w.T, preferred_element_type=jnp.float32)
    grad_g = hidden_grad * pre_up * sigmoid_gate * (1.0 + pre_gate * (1.0 - sigmoid_gate))
    grad_u = hidden_grad * active
    pre_grad = jnp.concatenate([grad_g, grad_u], axis=1).astype(jnp.bfloat16)
    row_grad = jnp.dot(pre_grad, gate_up_w.T, preferred_element_type=jnp.float32).astype(jnp.bfloat16)
    gate_up_part = jnp.dot(inputs.T, pre_grad, preferred_element_type=jnp.float32).astype(jnp.bfloat16)
    down_part = jnp.dot(hidden.T, out_grad, preferred_element_type=jnp.float32).astype(jnp.bfloat16)
    return (row_grad, gate_grad, gate_up_part, down_part)

def route_rows(routes_all):
    device_count = N_DP * N_EXPERT
    blocks = routes_all.reshape(device_count, TOK * 2)
    sources = jnp.arange(device_count, dtype=jnp.int32)
    onehot = (blocks[:, :, None] == jnp.arange(EXPERTS, dtype=jnp.int32)[None, None, :]).astype(jnp.int32)
    position = lax.optimization_barrier(jnp.sum((jnp.cumsum(onehot, axis=1) - onehot) * onehot, axis=2))
    replica = ((sources // N_EXPERT)[:, None] + position) % N_DP
    target = replica * N_EXPERT + blocks
    landing = sources[:, None] * CAP2 + position // N_DP
    return (target.reshape(-1).astype(jnp.int32), landing.reshape(-1).astype(jnp.int32))

def moe_forward(packed, routes_all, gate_up_s, down_s):
    target, landing = route_rows(routes_all)
    copies = jnp.repeat(packed, 2, axis=0)
    buffer_rows = N_DP * N_EXPERT * CAP2

    def visit(holding, device):
        matches = target == device
        landing_row = jnp.where(matches, landing, buffer_rows)
        buffer = jnp.zeros((buffer_rows, D), jnp.bfloat16).at[landing_row].set(copies, mode='drop')
        owner_index = device % N_EXPERT
        result = expert_forward(buffer, gate_up_s[owner_index], down_s[owner_index])
        picked = result[jnp.minimum(landing_row, buffer_rows - 1)]
        return (jnp.where(matches[:, None], picked, holding), None)
    final_state, ignored = lax.scan(visit, jnp.zeros_like(copies), jnp.arange(N_DP * N_EXPERT, dtype=jnp.int32))
    return final_state.reshape(TOKENS, 2, D)

def moe_backward(packed, upstream, weights_flat, routes_all, gate_up_s, down_s):
    target, landing = route_rows(routes_all)
    copies = jnp.repeat(packed, 2, axis=0)
    upstream_copies = jnp.repeat(upstream, 2, axis=0)
    buffer_rows = N_DP * N_EXPERT * CAP2

    def visit(holding, device):
        rows_state, gate_state, gate_up_acc, down_acc = holding
        matches = target == device
        landing_row = jnp.where(matches, landing, buffer_rows)
        buffer = jnp.zeros((buffer_rows, D), jnp.bfloat16).at[landing_row].set(copies, mode='drop')
        buffer_up = jnp.zeros((buffer_rows, D), jnp.bfloat16).at[landing_row].set(upstream_copies, mode='drop')
        buffer_weight = jnp.zeros((buffer_rows,), jnp.bfloat16).at[landing_row].set(weights_flat, mode='drop')
        owner_index = device % N_EXPERT
        row_grad, gate_grad, gate_up_part, down_part = expert_backward(buffer, buffer_up, buffer_weight, gate_up_s[owner_index], down_s[owner_index])
        clipped = jnp.minimum(landing_row, buffer_rows - 1)
        rows_state = jnp.where(matches[:, None], row_grad[clipped], rows_state)
        gate_state = jnp.where(matches, gate_grad[clipped], gate_state)
        gate_up_acc = gate_up_acc.at[owner_index].add(gate_up_part.astype(jnp.float32))
        down_acc = down_acc.at[owner_index].add(down_part.astype(jnp.float32))
        return ((rows_state, gate_state, gate_up_acc, down_acc), None)
    start = (jnp.zeros_like(copies), jnp.zeros((2 * TOKENS,), jnp.bfloat16), jnp.zeros((EXPERTS, D, 2 * FF), jnp.float32), jnp.zeros((EXPERTS, FF, D), jnp.float32))
    final_state, ignored = lax.scan(visit, start, jnp.arange(N_DP * N_EXPERT, dtype=jnp.int32))
    rows_state, gate_state, gate_up_acc, down_acc = final_state
    return (rows_state.reshape(TOKENS, 2, D), gate_state.reshape(TOKENS, 2), gate_up_acc, down_acc)

def reference(fresh, cotangent, prev_out, prev_grad, saved_in, route_fwd, route_bwd, router, gate_up, down):
    outputs_fwd = []
    outputs_bwd = []
    grads_gate_up = []
    grads_down = []
    grads_router = []
    for section_index in range(SECTIONS):
        inputs_fwd = fresh if section_index == 0 else prev_out[section_index - 1]
        upstream = cotangent if section_index == SECTIONS - 1 else prev_grad[section_index + 1]
        inputs_bwd = saved_in[section_index]
        router_w = router[section_index]
        unit_fwd, spread_fwd = normalize(inputs_fwd)
        packed_fwd = unit_fwd.astype(jnp.bfloat16)
        first_fwd, second_fwd, onehot_fwd = gate_pair(packed_fwd, router_w, route_fwd[section_index])
        chosen = moe_forward(packed_fwd, route_fwd[section_index], gate_up[section_index], down[section_index])
        section_value = inputs_fwd.astype(jnp.float32) + first_fwd[:, None] * chosen[:, 0].astype(jnp.float32) + second_fwd[:, None] * chosen[:, 1].astype(jnp.float32)
        outputs_fwd.append(section_value.astype(jnp.bfloat16))
        unit_bwd, spread_bwd = normalize(inputs_bwd)
        packed_bwd = unit_bwd.astype(jnp.bfloat16)
        first_bwd, second_bwd, onehot_bwd = gate_pair(packed_bwd, router_w, route_bwd[section_index])
        weights_flat = jnp.stack([first_bwd, second_bwd], axis=1).reshape(-1).astype(jnp.bfloat16)
        row_grads, gate_grads, gate_up_acc, down_acc = moe_backward(packed_bwd, upstream, weights_flat, route_bwd[section_index], gate_up[section_index], down[section_index])
        gate_float = gate_grads.astype(jnp.float32)
        logit_step = first_bwd * second_bwd * (gate_float[:, 0] - gate_float[:, 1])
        logit_grad = (onehot_bwd[:, 0, :] - onehot_bwd[:, 1, :]) * logit_step[:, None]
        normed_grad = row_grads[:, 0].astype(jnp.float32) + row_grads[:, 1].astype(jnp.float32)
        normed_grad = normed_grad + jnp.dot(logit_grad, router_w.astype(jnp.float32).T, precision=lax.Precision.HIGHEST)
        router_grad = jnp.dot(packed_bwd.astype(jnp.float32).T, logit_grad, precision=lax.Precision.HIGHEST)
        inner_mean = lax.optimization_barrier(jnp.mean(normed_grad * unit_bwd, axis=1, keepdims=True))
        grad_value = upstream.astype(jnp.float32) + (normed_grad - unit_bwd * inner_mean) / spread_bwd
        outputs_bwd.append(grad_value.astype(jnp.bfloat16))
        grads_gate_up.append(gate_up_acc.astype(jnp.bfloat16))
        grads_down.append(down_acc.astype(jnp.bfloat16))
        grads_router.append(router_grad)
    return (jnp.stack(outputs_fwd), jnp.stack(outputs_bwd), jnp.stack(grads_gate_up), jnp.stack(grads_down), jnp.stack(grads_router))
```

```python
import jax
import jax.numpy as jnp
from jax import lax
from jax.sharding import PartitionSpec as P

EPSILON = 1e-05


def passed_along(x, axis, by):
    length = lax.axis_size(axis)
    pairs = [(i, i + by) for i in range(length) if 0 <= i + by < length]
    return lax.ppermute(x, axis, pairs)


def dot(a, b, ca, cb):
    return lax.dot_general(a, b, (((ca,), (cb,)), ((), ())), preferred_element_type=jnp.float32)


def normalize(values_in):
    values = values_in.astype(jnp.float32)
    spread = jnp.sqrt(jnp.mean(values * values, axis=-1, keepdims=True) + EPSILON)
    return (values / spread, spread)


def gates(normed, router_w, routes):
    experts = router_w.shape[1]
    logits = jnp.dot(normed, router_w, preferred_element_type=jnp.float32)
    onehot = (routes[:, :, None] == jnp.arange(experts, dtype=jnp.int32)[None, None, :]).astype(
        jnp.float32
    )
    chosen = jnp.sum(onehot * logits[:, None, :], axis=2)
    first = jax.nn.sigmoid(chosen[:, 0] - chosen[:, 1])
    second = jax.nn.sigmoid(chosen[:, 1] - chosen[:, 0])
    return first, second, onehot


def shards(
    fresh, cotangent, prev_out, prev_grad, saved_in, route_fwd, route_bwd, router, gate_up, down
):
    section = lax.axis_index("pipe")
    sections = lax.axis_size("pipe")
    me = lax.axis_index("expert")
    arrived = passed_along(prev_out[0], "pipe", 1)
    returned = passed_along(prev_grad[0], "pipe", -1)
    inputs_fwd = jnp.where(section == 0, fresh, arrived)
    upstream = jnp.where(section == sections - 1, cotangent, returned)
    inputs_bwd = saved_in[0]
    router_w, gate_up_w, down_w = router[0], gate_up[0, 0], down[0, 0]
    width = down_w.shape[0]
    model = fresh.shape[1]
    experts = router_w.shape[1]

    def gather(x):
        return lax.all_gather(x, "expert", axis=0, tiled=True)

    def weights_for(normed, routes):
        first, second, onehot = gates(normed, router_w, routes)
        dense = onehot[:, 0, :] * first[:, None] + onehot[:, 1, :] * second[:, None]
        mine = (jnp.arange(experts) == me).astype(jnp.float32)
        return jnp.sum(dense * mine[None, :], axis=1)

    unit_bwd, spread_bwd = normalize(inputs_bwd)
    packed_bwd = unit_bwd.astype(jnp.bfloat16)
    all_bwd = gather(packed_bwd)
    all_up = gather(upstream)
    unit_fwd, _ = normalize(inputs_fwd)
    all_fwd = gather(unit_fwd.astype(jnp.bfloat16))
    routes_bwd = gather(route_bwd[0])
    routes_fwd = gather(route_fwd[0])

    weight = weights_for(all_bwd, routes_bwd)[:, None]
    pre = dot(all_bwd, gate_up_w, 1, 0)
    gate, up = pre[:, :width], pre[:, width:]
    sig = jax.nn.sigmoid(gate)
    active = gate * sig
    hidden = active * up
    up_down = dot(all_up, down_w, 1, 1)
    gate_grad = jnp.sum(hidden * up_down, axis=1, keepdims=True)
    hidden_grad = weight * up_down
    grad_g = hidden_grad * up * sig * (1.0 + gate * (1.0 - sig))
    grad_u = hidden_grad * active
    pre_grad = jnp.concatenate([grad_g, grad_u], axis=1).astype(jnp.bfloat16)
    row_grad = dot(pre_grad, gate_up_w, 1, 1).astype(jnp.bfloat16)
    mine = (jnp.arange(128) == me).astype(jnp.float32)[None, :]
    payload = jnp.concatenate([row_grad, (gate_grad * mine).astype(jnp.bfloat16)], axis=1)
    back = lax.psum_scatter(payload, "expert", scatter_dimension=0, tiled=True)
    gate_up_part = dot(all_bwd, pre_grad, 0, 0).astype(jnp.bfloat16)
    down_part = dot((weight * hidden).astype(jnp.bfloat16), all_up, 0, 0).astype(jnp.bfloat16)
    grad_gate_up = lax.psum_scatter(gate_up_part, "dp", scatter_dimension=0, tiled=True)
    grad_down = lax.psum_scatter(down_part, "dp", scatter_dimension=1, tiled=True)

    weight_f = weights_for(all_fwd, routes_fwd)[:, None]
    pre_f = dot(all_fwd, gate_up_w, 1, 0)
    gate_f, up_f = pre_f[:, :width], pre_f[:, width:]
    hidden_f = (gate_f * jax.nn.sigmoid(gate_f) * up_f).astype(jnp.bfloat16)
    y = (weight_f * dot(hidden_f, down_w, 1, 0)).astype(jnp.bfloat16)
    y_sum = lax.psum_scatter(y, "expert", scatter_dimension=0, tiled=True)
    section_out = (inputs_fwd.astype(jnp.float32) + y_sum.astype(jnp.float32)).astype(jnp.bfloat16)

    first, second, onehot = gates(packed_bwd, router_w, route_bwd[0])
    back_gate = back[:, model : model + experts].astype(jnp.float32)
    pair = onehot[:, 0, :] - onehot[:, 1, :]
    step = first * second * jnp.sum(pair * back_gate, axis=1)
    logit_grad = pair * step[:, None]
    normed_grad = back[:, :model].astype(jnp.float32) + lax.dot_general(
        logit_grad, router_w.astype(jnp.float32), (((1,), (1,)), ((), ())),
        precision=lax.Precision.HIGHEST,
    )
    router_part = lax.dot_general(
        logit_grad, packed_bwd.astype(jnp.float32), (((0,), (0,)), ((), ())),
        precision=lax.Precision.HIGHEST,
    )
    inner = jnp.mean(normed_grad * unit_bwd, axis=1, keepdims=True)
    grad_value = upstream.astype(jnp.float32) + (normed_grad - unit_bwd * inner) / spread_bwd
    input_grad = grad_value.astype(jnp.bfloat16)
    grad_router = lax.psum_scatter(router_part, ("dp", "expert"), scatter_dimension=1, tiled=True).T
    return (
        section_out[None],
        input_grad[None],
        grad_gate_up[None, None],
        grad_down[None, None],
        grad_router[None],
    )


def solution(mesh):
    tokens = P(("dp", "expert"), None)
    sectioned = P("pipe", ("dp", "expert"), None)
    return jax.shard_map(
        shards,
        mesh=mesh,
        in_specs=(
            tokens, tokens, sectioned, sectioned, sectioned, sectioned, sectioned,
            P("pipe", None, None),
            P("pipe", "expert", None, None),
            P("pipe", "expert", None, None),
        ),
        out_specs=(
            sectioned,
            sectioned,
            P("pipe", "expert", "dp", None),
            P("pipe", "expert", None, "dp"),
            sectioned,
        ),
        check_vma=False,
    )
```

```python
import functools

import jax
import jax.numpy as jnp
from jax import lax
from jax.experimental import pallas as pl
from jax.experimental.pallas import tpu as pltpu
from jax.sharding import PartitionSpec as P

EPSILON = 1e-05
MESH = pl.DeviceIdType.MESH
IDS = 16
STRIP = 16


def dot(a, b, ca, cb, precision=None):
    return lax.dot_general(
        a, b, (((ca,), (cb,)), ((), ())), precision=precision, preferred_element_type=jnp.float32
    )


class Gather:
    def __init__(self, view, send, recv, chips, x, c):
        self.view, self.send, self.recv = view, send, recv
        self.chips, self.x, self.c = chips, x, c

    def copy(self, block, at, target):
        ref = self.view(block)
        return pltpu.make_async_remote_copy(
            src_ref=ref, dst_ref=ref, send_sem=self.send.at[at], recv_sem=self.recv.at[at],
            device_id={"expert": target}, device_id_type=MESH,
        )

    def here(self, i, core):
        return lax.rem(self.x + self.chips - i, self.chips) * 2 + core

    def start(self):
        own = self.x * 2 + self.c
        for i in range(1, self.chips):
            self.copy(own, i, lax.rem(self.x + i, self.chips) * 2 + self.c).start()
        self.copy(own, 0, self.x * 2 + 1 - self.c).start()

    def forward(self):
        other = self.x * 2 + 1 - self.c
        for i in range(1, self.chips):
            self.copy(self.here(i, self.c), i, other).wait_recv()
            self.copy(self.here(i, self.c), self.chips - 1 + i, other).start()

    def finish(self):
        other = self.x * 2 + 1 - self.c
        self.copy(other, 0, other).wait_recv()
        for i in range(1, self.chips):
            self.copy(self.here(i, 1 - self.c), self.chips - 1 + i, other).wait_recv()

    def sent(self):
        other = self.x * 2 + 1 - self.c
        own = self.x * 2 + self.c
        self.copy(own, 0, other).wait_send()
        for i in range(1, self.chips):
            self.copy(own, i, other).wait_send()
            self.copy(self.here(i, self.c), self.chips - 1 + i, other).wait_send()


class Scatter:
    def __init__(self, view, pair, cross, sems, chips, x, c):
        self.view, self.pair, self.cross = view, pair, cross
        self.pair_send, self.pair_recv, self.cross_send, self.cross_recv = sems
        self.chips, self.x, self.c = chips, x, c

    def pair_copy(self, i):
        to = lax.rem(self.x + i, self.chips) * 2 + 1 - self.c
        return pltpu.make_async_remote_copy(
            src_ref=self.view(to), dst_ref=self.pair.at[i],
            send_sem=self.pair_send.at[i], recv_sem=self.pair_recv.at[i],
            device_id={"expert": self.x * 2 + 1 - self.c}, device_id_type=MESH,
        )

    def cross_copy(self, i):
        return pltpu.make_async_remote_copy(
            src_ref=self.pair.at[i], dst_ref=self.cross.at[i - 1],
            send_sem=self.cross_send.at[i - 1], recv_sem=self.cross_recv.at[i - 1],
            device_id={"expert": lax.rem(self.x + i, self.chips) * 2 + self.c}, device_id_type=MESH,
        )

    def order(self):
        return list(range(1, self.chips)) + [0]

    def start(self):
        for i in self.order():
            self.pair_copy(i).start()

    def forward(self):
        for i in range(1, self.chips):
            self.pair_copy(i).wait_recv()
            mine = self.view(lax.rem(self.x + i, self.chips) * 2 + self.c)

            def add(k, carry, i=i, mine=mine):
                rows = pl.ds(pl.multiple_of(k * STRIP, STRIP), STRIP)
                self.pair[i, rows, :] = (
                    self.pair[i, rows, :].astype(jnp.float32) + mine[rows, :].astype(jnp.float32)
                ).astype(jnp.bfloat16)
                return carry

            lax.fori_loop(0, self.pair.shape[1] // STRIP, add, 0)
            self.cross_copy(i).start()

    def finish(self):
        self.pair_copy(0).wait_recv()
        for i in range(1, self.chips):
            self.cross_copy(i).wait_recv()

    def total(self, rows):
        value = self.view(self.x * 2 + self.c)[rows, :].astype(jnp.float32)
        value = value + self.pair[0, rows, :].astype(jnp.float32)
        for i in range(1, self.chips):
            value = value + self.cross[i - 1, rows, :].astype(jnp.float32)
        return value

    def sent(self):
        for i in range(self.chips):
            self.pair_copy(i).wait_send()
        for i in range(1, self.chips):
            self.cross_copy(i).wait_send()


def kernel(
    dims,
    fresh, cotangent, prev_out, prev_grad, saved_in, lanes_fwd, lanes_bwd, router_b, router_f,
    gate_up, down,
    section_out, input_grad, grad_gate_up, grad_down, grad_router,
    all_bwd, all_fwd, all_up, part, pair_row, cross_row, pair_y, cross_y,
    gate_up_w, down_w, saved, inputs_fwd, gu_send, gu_recv, dn_send, dn_recv, rt_send, rt_recv,
    gates_all, pre_acc, log_acc, hid_acc, grad_pre, hid_weighted, logit_ref, rt_own,
    local_sem, pipe_send, pipe_recv, g_send, g_recv, s_psend, s_precv, s_csend, s_crecv,
    gu_ss, gu_rs, dn_ss, dn_rs, rt_ss, rt_rs,
):
    sections, replicas, owners = dims
    tokens, model = saved.shape
    width = down_w.shape[0]
    experts = owners
    chips = owners // 2
    total = owners * tokens
    piece = model // replicas
    chunk = gu_send.shape[2]
    steps = gu_send.shape[1]
    rt_width = rt_own.shape[1]
    rt_step = rt_width if rt_width < piece else 0

    section = lax.axis_index("pipe")
    dp = lax.axis_index("dp")
    me = lax.axis_index("expert")
    x, c = me // 2, lax.rem(me, 2)
    has_prev = section > 0
    has_next = section < sections - 1
    own_rows = pl.ds(pl.multiple_of(me * tokens, tokens), tokens)

    load_saved = pltpu.make_async_copy(saved_in, saved, local_sem.at[0])
    load_gate = pltpu.make_async_copy(gate_up, gate_up_w, local_sem.at[1])
    load_down = pltpu.make_async_copy(down, down_w, local_sem.at[2])
    load_fresh = pltpu.make_async_copy(fresh, inputs_fwd, local_sem.at[3])
    load_cot = pltpu.make_async_copy(cotangent, all_up.at[own_rows], local_sem.at[4])
    load_saved.start()
    load_gate.start()
    load_down.start()

    barrier = pltpu.get_barrier_semaphore()

    @pl.when(has_prev)
    def _():
        pl.semaphore_signal(barrier, inc=1, device_id={"pipe": section - 1}, device_id_type=MESH)

    @pl.when(has_next)
    def _():
        pl.semaphore_signal(barrier, inc=1, device_id={"pipe": section + 1}, device_id_type=MESH)

    pl.semaphore_signal(barrier, inc=1, device_id={"expert": x * 2 + 1 - c}, device_id_type=MESH)
    for i in range(1, chips):
        pl.semaphore_signal(
            barrier, inc=1, device_id={"expert": lax.rem(x + i, chips) * 2 + c}, device_id_type=MESH
        )
    for i in range(1, replicas):
        pl.semaphore_signal(
            barrier, inc=1, device_id={"dp": lax.rem(dp + i, replicas)}, device_id_type=MESH
        )

    def strips(body):
        def step(k, carry):
            body(pl.multiple_of(k * STRIP, STRIP))
            return carry

        lax.fori_loop(0, tokens // STRIP, step, 0)

    def inverse(values):
        return 1.0 / jnp.sqrt(jnp.mean(values * values, axis=1, keepdims=True) + EPSILON)

    def normalize_into(source, target, lanes):
        def body(at):
            values = source[pl.ds(at, STRIP), :].astype(jnp.float32)
            rows = pl.ds(pl.multiple_of(me * tokens + at, STRIP), STRIP)
            target[rows, :model] = (values * inverse(values)).astype(jnp.bfloat16)
            target[rows, model:] = lanes[pl.ds(at, STRIP), :]

        strips(body)

    load_saved.wait()
    normalize_into(saved, all_bwd, lanes_bwd)
    pl.semaphore_wait(
        barrier,
        chips + replicas - 1 + jnp.minimum(section, 1) + jnp.minimum(sections - 1 - section, 1),
    )

    send_out = pltpu.make_async_remote_copy(
        src_ref=prev_out, dst_ref=inputs_fwd, send_sem=pipe_send.at[0], recv_sem=pipe_recv.at[0],
        device_id={"pipe": lax.rem(section + 1, sections)}, device_id_type=MESH,
    )
    send_grad = pltpu.make_async_remote_copy(
        src_ref=prev_grad, dst_ref=all_up.at[own_rows],
        send_sem=pipe_send.at[1], recv_sem=pipe_recv.at[1],
        device_id={"pipe": lax.rem(section + sections - 1, sections)}, device_id_type=MESH,
    )

    @pl.when(has_prev)
    def _():
        send_grad.start()

    @pl.when(has_next)
    def _():
        send_out.start()

    @pl.when(jnp.logical_not(has_prev))
    def _():
        load_fresh.start()

    @pl.when(jnp.logical_not(has_next))
    def _():
        load_cot.start()

    def block_of(ref):
        return lambda j: ref.at[pl.ds(pl.multiple_of(j * tokens, tokens), tokens)]

    gather_bwd = Gather(block_of(all_bwd), g_send.at[0], g_recv.at[0], chips, x, c)
    gather_up = Gather(block_of(all_up), g_send.at[1], g_recv.at[1], chips, x, c)
    gather_fwd = Gather(block_of(all_fwd), g_send.at[2], g_recv.at[2], chips, x, c)
    gather_gate = Gather(lambda j: gates_all.at[j], g_send.at[3], g_recv.at[3], chips, x, c)
    sems = [
        tuple(ref.at[a] for ref in (s_psend, s_precv, s_csend, s_crecv)) for a in range(2)
    ]
    scatter_row = Scatter(block_of(part), pair_row, cross_row, sems[0], chips, x, c)

    def narrow(j):
        return all_bwd.at[pl.ds(pl.multiple_of(j * tokens, tokens), tokens), pl.ds(0, model)]

    scatter_y = Scatter(narrow, pair_y, cross_y, sems[1], chips, x, c)

    def columns(k):
        return pl.ds(pl.multiple_of(k * chunk, chunk), chunk)

    def chunks(body):
        def step(k, carry):
            body(columns(k))
            return carry

        lax.fori_loop(0, model // chunk, step, 0)

    lane = lax.broadcasted_iota(jnp.int32, (total, IDS), 1).astype(jnp.float32)
    mine = (lane == me.astype(jnp.float32)).astype(jnp.float32)

    def project(rows_ref):
        pre_acc[...] = jnp.zeros_like(pre_acc)
        log_acc[...] = jnp.zeros_like(log_acc)

        def body(cols):
            rows = rows_ref[:, cols]
            pre_acc[...] += dot(rows, gate_up_w[cols, :], 1, 0)
            log_acc[...] += dot(rows, router_b[:, cols], 1, 1)

        chunks(body)
        ids = rows_ref[:, model:].astype(jnp.float32)
        one = (lane == ids[:, 0:1]).astype(jnp.float32)
        two = (lane == ids[:, 1:2]).astype(jnp.float32)
        logits = log_acc[...]
        apart = jnp.sum((one - two) * logits, axis=1, keepdims=True)
        first, second = jax.nn.sigmoid(apart), jax.nn.sigmoid(-apart)
        weight = jnp.sum((one * first + two * second) * mine, axis=1, keepdims=True)
        return one, two, first, second, weight, pre_acc[:, :width], pre_acc[:, width:]

    gather_bwd.start()

    @pl.when(has_next)
    def _():
        send_grad.wait_recv()

    @pl.when(jnp.logical_not(has_next))
    def _():
        load_cot.wait()

    gather_up.start()
    gather_bwd.forward()

    @pl.when(has_prev)
    def _():
        send_out.wait_recv()

    @pl.when(jnp.logical_not(has_prev))
    def _():
        load_fresh.wait()

    normalize_into(inputs_fwd, all_fwd, lanes_fwd)
    load_gate.wait()
    load_down.wait()
    gather_bwd.finish()
    one, two, first, second, weight, gate, up = project(all_bwd)
    sig = jax.nn.sigmoid(gate)
    active = gate * sig
    hidden = active * up
    hid_weighted[...] = (weight * hidden).astype(jnp.bfloat16)

    gather_up.forward()
    gather_fwd.start()
    gather_up.finish()
    hid_acc[...] = jnp.zeros_like(hid_acc)

    def up_body(cols):
        hid_acc[...] += dot(all_up[:, cols], down_w[:, cols], 1, 1)

    chunks(up_body)
    up_down = hid_acc[...]
    gate_grad = jnp.sum(hidden * up_down, axis=1, keepdims=True)
    lanes = lax.broadcasted_iota(jnp.int32, (total, 128), 1).astype(jnp.float32)
    gates_all[me] = (gate_grad * (lanes == me.astype(jnp.float32)).astype(jnp.float32)).astype(
        jnp.bfloat16
    )
    gather_gate.start()
    hidden_grad = weight * up_down
    grad_pre[:, :width] = (hidden_grad * up * sig * (1.0 + gate * (1.0 - sig))).astype(jnp.bfloat16)
    grad_pre[:, width:] = (hidden_grad * active).astype(jnp.bfloat16)

    def gu_copy(i, k):
        return pltpu.make_async_remote_copy(
            src_ref=gu_send.at[i - 1, k], dst_ref=gu_recv.at[i - 1, k],
            send_sem=gu_ss.at[i - 1, k], recv_sem=gu_rs.at[i - 1, k],
            device_id={"dp": lax.rem(dp + i, replicas)}, device_id_type=MESH,
        )

    def dn_copy(i, k):
        return pltpu.make_async_remote_copy(
            src_ref=dn_send.at[i - 1, k], dst_ref=dn_recv.at[i - 1, k],
            send_sem=dn_ss.at[i - 1, k], recv_sem=dn_rs.at[i - 1, k],
            device_id={"dp": lax.rem(dp + i, replicas)}, device_id_type=MESH,
        )

    def weight_parts(owner, k):
        cols = pl.ds(pl.multiple_of(owner * piece + k * chunk, chunk), chunk)
        gu = dot(all_bwd[:, cols], grad_pre[...], 0, 0).astype(jnp.bfloat16)
        dn = dot(hid_weighted[...], all_up[:, cols], 0, 0).astype(jnp.bfloat16)
        return gu, dn

    for i in range(1, replicas):
        def send_step(k, carry, i=i):
            gu, dn = weight_parts(lax.rem(dp + i, replicas), k)
            gu_send[i - 1, k] = gu
            dn_send[i - 1, k] = dn
            gu_copy(i, k).start()
            dn_copy(i, k).start()
            return carry

        lax.fori_loop(0, steps, send_step, 0)

    def row_body(cols):
        part[:, cols] = dot(grad_pre[...], gate_up_w[cols, :], 1, 1).astype(jnp.bfloat16)

    chunks(row_body)
    scatter_row.start()

    def own_step(k, carry):
        gu, dn = weight_parts(dp, k)
        grad_gate_up[columns(k), :] = gu
        grad_down[:, columns(k)] = dn
        return carry

    gather_gate.forward()
    scatter_row.forward()
    lax.fori_loop(0, steps, own_step, 0)

    gather_gate.finish()
    gate_all = gates_all[0].astype(jnp.float32)
    for j in range(1, owners):
        gate_all = gate_all + gates_all[j].astype(jnp.float32)
    logit = (one - two) * (
        first * second * jnp.sum((one - two) * gate_all[:, :IDS], axis=1, keepdims=True)
    )
    logit_ref[...] = logit

    def rt_copy(i):
        return pltpu.make_async_remote_copy(
            src_ref=rt_send.at[i - 1], dst_ref=rt_recv.at[i - 1],
            send_sem=rt_ss.at[i - 1], recv_sem=rt_rs.at[i - 1],
            device_id={"dp": lax.rem(dp + i, replicas)}, device_id_type=MESH,
        )

    def router_part(owner):
        cols = pl.ds(pl.multiple_of(owner * piece + me * rt_step, 128), rt_width)
        return dot(
            logit_ref[...], all_bwd[:, cols].astype(jnp.float32), 0, 0, lax.Precision.HIGHEST
        )

    for i in range(1, replicas):
        rt_send[i - 1] = router_part(lax.rem(dp + i, replicas))
        rt_copy(i).start()
    rt_own[...] = router_part(dp)

    gather_fwd.forward()
    gather_fwd.finish()
    gather_bwd.sent()
    _, _, _, _, weight_f, gate_f, up_f = project(all_fwd)
    hid_weighted[...] = (weight_f * (gate_f * jax.nn.sigmoid(gate_f) * up_f)).astype(jnp.bfloat16)

    def y_body(cols):
        all_bwd[:, cols] = dot(hid_weighted[...], down_w[:, cols], 1, 0).astype(jnp.bfloat16)

    chunks(y_body)
    scatter_y.start()
    scatter_y.forward()

    scatter_row.finish()

    def grad_body(at):
        rows = pl.ds(at, STRIP)
        home = pl.ds(pl.multiple_of(me * tokens + at, STRIP), STRIP)
        values = saved[rows, :].astype(jnp.float32)
        inv = inverse(values)
        unit = values * inv
        normed_grad = scatter_row.total(rows)
        steps_here = logit_ref[home, :]
        for j in range(experts):
            normed_grad = normed_grad + steps_here[:, j : j + 1] * router_f[j : j + 1, :]
        inner = jnp.mean(normed_grad * unit, axis=1, keepdims=True)
        input_grad[rows, :] = (
            all_up[home, :].astype(jnp.float32) + (normed_grad - unit * inner) * inv
        ).astype(jnp.bfloat16)

    strips(grad_body)

    rt = rt_own[...]
    for i in range(1, replicas):
        rt_copy(i).wait_recv()
        rt = rt + rt_recv[i - 1]
    grad_router[...] = rt

    for i in range(1, replicas):
        def add_step(k, carry, i=i):
            gu_copy(i, k).wait_recv()
            dn_copy(i, k).wait_recv()
            cols = columns(k)
            grad_gate_up[cols, :] = (
                grad_gate_up[cols, :].astype(jnp.float32) + gu_recv[i - 1, k].astype(jnp.float32)
            ).astype(jnp.bfloat16)
            grad_down[:, cols] = (
                grad_down[:, cols].astype(jnp.float32) + dn_recv[i - 1, k].astype(jnp.float32)
            ).astype(jnp.bfloat16)
            return carry

        lax.fori_loop(0, steps, add_step, 0)

    scatter_y.finish()

    def out_body(at):
        rows = pl.ds(at, STRIP)
        section_out[rows, :] = (
            inputs_fwd[rows, :].astype(jnp.float32) + scatter_y.total(rows)
        ).astype(jnp.bfloat16)

    strips(out_body)

    @pl.when(has_prev)
    def _():
        send_grad.wait_send()

    @pl.when(has_next)
    def _():
        send_out.wait_send()

    gather_up.sent()
    gather_fwd.sent()
    gather_gate.sent()
    scatter_row.sent()
    scatter_y.sent()
    for i in range(1, replicas):
        rt_copy(i).wait_send()

        def drain(k, carry, i=i):
            gu_copy(i, k).wait_send()
            dn_copy(i, k).wait_send()
            return carry

        lax.fori_loop(0, steps, drain, 0)


def shards(
    fresh, cotangent, prev_out, prev_grad, saved_in, route_fwd, route_bwd, router, gate_up, down
):
    sections = lax.axis_size("pipe")
    replicas = lax.axis_size("dp")
    owners = lax.axis_size("expert")
    tokens, model = fresh.shape
    width = down.shape[2]
    experts = router.shape[2]
    chips = owners // 2
    total = owners * tokens
    piece = model // replicas
    chunk = min(768, piece)
    steps = piece // chunk
    rt_width = piece // owners if (piece // owners) % 128 == 0 else piece

    def lanes(routes):
        return jnp.pad(routes[0].astype(jnp.bfloat16), ((0, 0), (0, 126)))

    router_f = jnp.pad(router[0].T.astype(jnp.float32), ((0, IDS - experts), (0, 0)))
    bf16, f32 = jnp.bfloat16, jnp.float32
    far = max(replicas - 1, 1)
    dma = pltpu.SemaphoreType.DMA
    any_spec = pl.BlockSpec(memory_space=pl.ANY)
    vmem = pl.BlockSpec(memory_space=pltpu.VMEM)
    outs = pl.pallas_call(
        functools.partial(kernel, (sections, replicas, owners)),
        out_shape=(
            jax.ShapeDtypeStruct((tokens, model), bf16),
            jax.ShapeDtypeStruct((tokens, model), bf16),
            jax.ShapeDtypeStruct((piece, 2 * width), bf16),
            jax.ShapeDtypeStruct((width, piece), bf16),
            jax.ShapeDtypeStruct((IDS, rt_width), f32),
        ),
        in_specs=[any_spec] * 5 + [vmem] * 4 + [any_spec] * 2,
        out_specs=(vmem,) * 5,
        scratch_shapes=[
            pltpu.VMEM((total, model + 128), bf16),
            pltpu.VMEM((total, model + 128), bf16),
            pltpu.VMEM((total, model), bf16),
            pltpu.VMEM((total, model), bf16),
            pltpu.VMEM((chips, tokens, model), bf16),
            pltpu.VMEM((chips - 1, tokens, model), bf16),
            pltpu.VMEM((chips, tokens, model), bf16),
            pltpu.VMEM((chips - 1, tokens, model), bf16),
            pltpu.VMEM((model, 2 * width), bf16),
            pltpu.VMEM((width, model), bf16),
            pltpu.VMEM((tokens, model), bf16),
            pltpu.VMEM((tokens, model), bf16),
            pltpu.VMEM((far, steps, chunk, 2 * width), bf16),
            pltpu.VMEM((far, steps, chunk, 2 * width), bf16),
            pltpu.VMEM((far, steps, width, chunk), bf16),
            pltpu.VMEM((far, steps, width, chunk), bf16),
            pltpu.VMEM((far, IDS, rt_width), f32),
            pltpu.VMEM((far, IDS, rt_width), f32),
            pltpu.VMEM((owners, total, 128), bf16),
            pltpu.VMEM((total, 2 * width), f32),
            pltpu.VMEM((total, IDS), f32),
            pltpu.VMEM((total, width), f32),
            pltpu.VMEM((total, 2 * width), bf16),
            pltpu.VMEM((total, width), bf16),
            pltpu.VMEM((total, IDS), f32),
            pltpu.VMEM((IDS, rt_width), f32),
            dma((5,)),
            dma((2,)),
            dma((2,)),
            dma((4, 2 * chips - 1)),
            dma((4, 2 * chips - 1)),
            dma((2, chips)),
            dma((2, chips)),
            dma((2, chips - 1)),
            dma((2, chips - 1)),
            dma((far, steps)),
            dma((far, steps)),
            dma((far, steps)),
            dma((far, steps)),
            dma((far,)),
            dma((far,)),
        ],
        compiler_params=pltpu.CompilerParams(
            collective_id=0, has_side_effects=True, vmem_limit_bytes=62 * 2**20
        ),
        name="relay_step",
    )(
        fresh, cotangent, prev_out[0], prev_grad[0], saved_in[0], lanes(route_fwd),
        lanes(route_bwd), router_f.astype(bf16), router_f, gate_up[0, 0], down[0, 0],
    )
    section_out, input_grad, grad_gate_up, grad_down, grad_router = outs
    share = piece // owners
    if rt_width != share:
        grad_router = lax.dynamic_slice_in_dim(
            grad_router, lax.axis_index("expert") * share, share, axis=1
        )
    return (
        section_out[None],
        input_grad[None],
        grad_gate_up[None, None],
        grad_down[None, None],
        grad_router[:experts].T[None],
    )


def solution(mesh):
    tokens = P(("dp", "expert"), None)
    sectioned = P("pipe", ("dp", "expert"), None)
    return jax.shard_map(
        shards,
        mesh=mesh,
        in_specs=(
            tokens, tokens, sectioned, sectioned, sectioned, sectioned, sectioned,
            P("pipe", None, None),
            P("pipe", "expert", None, None),
            P("pipe", "expert", None, None),
        ),
        out_specs=(
            sectioned,
            sectioned,
            P("pipe", "expert", "dp", None),
            P("pipe", "expert", None, "dp"),
            sectioned,
        ),
        check_vma=False,
    )
```

```python
import functools

import jax
import jax.numpy as jnp
from jax import lax
from jax.experimental import pallas as pl
from jax.experimental.pallas import tpu as pltpu
from jax.sharding import PartitionSpec as P

EPSILON = 1e-05
MESH = pl.DeviceIdType.MESH
STRIP = 16


def dot(a, b, ca, cb, precision=None):
    return lax.dot_general(
        a, b, (((ca,), (cb,)), ((), ())), precision=precision, preferred_element_type=jnp.float32
    )


class Gather:
    def __init__(self, view, send, recv, chips, x, c):
        self.view, self.send, self.recv = view, send, recv
        self.chips, self.x, self.c = chips, x, c

    def copy(self, block, at, target):
        ref = self.view(block)
        return pltpu.make_async_remote_copy(
            src_ref=ref, dst_ref=ref, send_sem=self.send.at[at], recv_sem=self.recv.at[at],
            device_id={"expert": target}, device_id_type=MESH,
        )

    def here(self, i, core):
        return lax.rem(self.x + self.chips - i, self.chips) * 2 + core

    def start(self):
        own = self.x * 2 + self.c
        for i in range(1, self.chips):
            self.copy(own, i, lax.rem(self.x + i, self.chips) * 2 + self.c).start()
        self.copy(own, 0, self.x * 2 + 1 - self.c).start()

    def crossed(self):
        for i in range(1, self.chips):
            self.copy(self.here(i, self.c), i, self.x * 2 + 1 - self.c).wait_recv()

    def pass_on(self):
        other = self.x * 2 + 1 - self.c
        for i in range(1, self.chips):
            self.copy(self.here(i, self.c), self.chips - 1 + i, other).start()

    def forward(self):
        self.crossed()
        self.pass_on()

    def finish(self):
        other = self.x * 2 + 1 - self.c
        self.copy(other, 0, other).wait_recv()
        for i in range(1, self.chips):
            self.copy(self.here(i, 1 - self.c), self.chips - 1 + i, other).wait_recv()

    def sent(self):
        other = self.x * 2 + 1 - self.c
        own = self.x * 2 + self.c
        self.copy(own, 0, other).wait_send()
        for i in range(1, self.chips):
            self.copy(own, i, other).wait_send()
            self.copy(self.here(i, self.c), self.chips - 1 + i, other).wait_send()


class Scatter:
    def __init__(self, view, pair, cross, sems, chips, x, c):
        self.view, self.pair, self.cross = view, pair, cross
        self.pair_send, self.pair_recv, self.cross_send, self.cross_recv = sems
        self.chips, self.x, self.c = chips, x, c

    def pair_copy(self, i):
        to = lax.rem(self.x + i, self.chips) * 2 + 1 - self.c
        return pltpu.make_async_remote_copy(
            src_ref=self.view(to), dst_ref=self.pair.at[i],
            send_sem=self.pair_send.at[i], recv_sem=self.pair_recv.at[i],
            device_id={"expert": self.x * 2 + 1 - self.c}, device_id_type=MESH,
        )

    def cross_copy(self, i):
        return pltpu.make_async_remote_copy(
            src_ref=self.pair.at[i], dst_ref=self.cross.at[i - 1],
            send_sem=self.cross_send.at[i - 1], recv_sem=self.cross_recv.at[i - 1],
            device_id={"expert": lax.rem(self.x + i, self.chips) * 2 + self.c}, device_id_type=MESH,
        )

    def order(self):
        return list(range(1, self.chips)) + [0]

    def start(self):
        for i in self.order():
            self.pair_copy(i).start()

    def forward(self):
        for i in range(1, self.chips):
            self.pair_copy(i).wait_recv()
            mine = self.view(lax.rem(self.x + i, self.chips) * 2 + self.c)

            def add(k, carry, i=i, mine=mine):
                rows = pl.ds(pl.multiple_of(k * STRIP, STRIP), STRIP)
                self.pair[i, rows, :] = (
                    self.pair[i, rows, :].astype(jnp.float32) + mine[rows, :].astype(jnp.float32)
                ).astype(jnp.bfloat16)
                return carry

            lax.fori_loop(0, self.pair.shape[1] // STRIP, add, 0)
            self.cross_copy(i).start()

    def finish(self):
        self.pair_copy(0).wait_recv()
        for i in range(1, self.chips):
            self.cross_copy(i).wait_recv()

    def total(self, rows):
        value = self.view(self.x * 2 + self.c)[rows, :].astype(jnp.float32)
        value = value + self.pair[0, rows, :].astype(jnp.float32)
        for i in range(1, self.chips):
            value = value + self.cross[i - 1, rows, :].astype(jnp.float32)
        return value

    def sent(self):
        for i in range(self.chips):
            self.pair_copy(i).wait_send()
        for i in range(1, self.chips):
            self.cross_copy(i).wait_send()


def kernel(
    dims,
    fresh, cotangent, prev_out, prev_grad, saved_in, ids_bwd, ids_fwd, router_b,
    gate_up, down,
    section_out, input_grad, grad_gate_up, grad_down, grad_router,
    all_bwd, all_fwd, all_up, part, pair_row, cross_row, pair_y, cross_y,
    gate_up_w, down_w, saved, inputs_fwd, gu_send, gu_recv, dn_send, dn_recv, rt_send, rt_recv,
    gates_all, pre_acc, log_acc, hid_acc, grad_pre, hid_weighted, logit_ref, rt_own,
    local_sem, pipe_send, pipe_recv, g_send, g_recv, s_psend, s_precv, s_csend, s_crecv,
    gu_ss, gu_rs, dn_ss, dn_rs, rt_ss, rt_rs,
):
    sections, replicas, owners = dims
    tokens, model = saved.shape
    width = down_w.shape[0]
    experts = router_b.shape[0]
    half = tokens // 2
    chips = owners // 2
    total = owners * tokens
    piece = model // replicas
    chunk = gu_send.shape[2]
    steps = gu_send.shape[1]
    rt_width = rt_own.shape[1]
    rt_step = rt_width if rt_width < piece else 0

    section = lax.axis_index("pipe")
    dp = lax.axis_index("dp")
    me = lax.axis_index("expert")
    x, c = me // 2, lax.rem(me, 2)
    has_prev = section > 0
    has_next = section < sections - 1
    own_rows = pl.ds(pl.multiple_of(me * tokens, tokens), tokens)

    load_saved = pltpu.make_async_copy(saved_in, saved, local_sem.at[0])
    load_gate = pltpu.make_async_copy(gate_up, gate_up_w, local_sem.at[1])
    load_down = pltpu.make_async_copy(down, down_w, local_sem.at[2])
    load_fresh = pltpu.make_async_copy(fresh, inputs_fwd, local_sem.at[3])
    load_cot = pltpu.make_async_copy(cotangent, all_up.at[own_rows], local_sem.at[4])
    load_saved.start()
    load_gate.start()
    load_down.start()

    barrier = pltpu.get_barrier_semaphore()

    @pl.when(has_prev)
    def _():
        pl.semaphore_signal(barrier, inc=1, device_id={"pipe": section - 1}, device_id_type=MESH)

    @pl.when(has_next)
    def _():
        pl.semaphore_signal(barrier, inc=1, device_id={"pipe": section + 1}, device_id_type=MESH)

    pl.semaphore_signal(barrier, inc=1, device_id={"expert": x * 2 + 1 - c}, device_id_type=MESH)
    for i in range(1, chips):
        pl.semaphore_signal(
            barrier, inc=1, device_id={"expert": lax.rem(x + i, chips) * 2 + c}, device_id_type=MESH
        )
    for i in range(1, replicas):
        pl.semaphore_signal(
            barrier, inc=1, device_id={"dp": lax.rem(dp + i, replicas)}, device_id_type=MESH
        )

    def strips(body):
        def step(k, carry):
            body(pl.multiple_of(k * STRIP, STRIP))
            return carry

        lax.fori_loop(0, tokens // STRIP, step, 0)

    def inverse(values):
        return 1.0 / jnp.sqrt(jnp.mean(values * values, axis=1, keepdims=True) + EPSILON)

    def normalize_into(source, target, part_at):
        def step(k, carry):
            at = pl.multiple_of(part_at * half + k * STRIP, STRIP)
            values = source[pl.ds(at, STRIP), :].astype(jnp.float32)
            rows = pl.ds(pl.multiple_of(me * tokens + at, STRIP), STRIP)
            target[rows, :model] = (values * inverse(values)).astype(jnp.bfloat16)
            return carry

        lax.fori_loop(0, half // STRIP, step, 0)

    load_saved.wait()
    spot = lax.broadcasted_iota(jnp.int32, (2, 128), 0)
    slot = lax.broadcasted_iota(jnp.int32, (2, 128), 1)
    all_bwd[own_rows, model:] = (
        dot(ids_bwd[...].astype(jnp.float32), (slot == spot).astype(jnp.float32), 0, 0)
        + dot(ids_fwd[...].astype(jnp.float32), (slot == spot + 2).astype(jnp.float32), 0, 0)
    ).astype(jnp.bfloat16)
    normalize_into(saved, all_bwd, 0)
    pl.semaphore_wait(
        barrier,
        chips + replicas - 1 + jnp.minimum(section, 1) + jnp.minimum(sections - 1 - section, 1),
    )

    def relay_out(h):
        rows = pl.ds(h * half, half)
        return pltpu.make_async_remote_copy(
            src_ref=prev_out.at[rows], dst_ref=inputs_fwd.at[rows],
            send_sem=pipe_send.at[0, h], recv_sem=pipe_recv.at[0, h],
            device_id={"pipe": lax.rem(section + 1, sections)}, device_id_type=MESH,
        )

    def relay_grad(h):
        rows = pl.ds(pl.multiple_of(me * tokens + h * half, half), half)
        return pltpu.make_async_remote_copy(
            src_ref=prev_grad.at[pl.ds(h * half, half)], dst_ref=all_up.at[rows],
            send_sem=pipe_send.at[1, h], recv_sem=pipe_recv.at[1, h],
            device_id={"pipe": lax.rem(section + sections - 1, sections)}, device_id_type=MESH,
        )

    @pl.when(has_prev)
    def _():
        for h in range(2):
            relay_grad(h).start()

    @pl.when(has_next)
    def _():
        for h in range(2):
            relay_out(h).start()

    @pl.when(jnp.logical_not(has_prev))
    def _():
        load_fresh.start()

    @pl.when(jnp.logical_not(has_next))
    def _():
        load_cot.start()

    def block_of(ref):
        return lambda j: ref.at[pl.ds(pl.multiple_of(j * tokens, tokens), tokens)]

    def halves(ref, a):
        def view(h):
            return lambda j: ref.at[pl.ds(pl.multiple_of(j * tokens + h * half, half), half)]

        return [
            Gather(view(h), g_send.at[2 * a + h], g_recv.at[2 * a + h], chips, x, c)
            for h in range(2)
        ]

    gather_bwd = halves(all_bwd, 0)
    gather_up = halves(all_up, 1)
    gather_fwd = halves(all_fwd, 2)
    gather_gate = Gather(lambda j: gates_all.at[j], g_send.at[6], g_recv.at[6], chips, x, c)
    sems = [
        tuple(ref.at[a] for ref in (s_psend, s_precv, s_csend, s_crecv)) for a in range(2)
    ]
    scatter_row = Scatter(block_of(part), pair_row, cross_row, sems[0], chips, x, c)

    def narrow(j):
        return all_bwd.at[pl.ds(pl.multiple_of(j * tokens, tokens), tokens), pl.ds(0, model)]

    scatter_y = Scatter(narrow, pair_y, cross_y, sems[1], chips, x, c)

    def columns(k):
        return pl.ds(pl.multiple_of(k * chunk, chunk), chunk)

    def chunks(body):
        def step(k, carry):
            body(columns(k))
            return carry

        lax.fori_loop(0, model // chunk, step, 0)

    lane = lax.broadcasted_iota(jnp.int32, (total, experts), 1).astype(jnp.float32)
    mine = (lane == me.astype(jnp.float32)).astype(jnp.float32)

    def project(rows_ref, at):
        pre_acc[...] = jnp.zeros_like(pre_acc)
        log_acc[...] = jnp.zeros_like(log_acc)

        def body(cols):
            rows = rows_ref[:, cols]
            pre_acc[...] += dot(rows, gate_up_w[cols, :], 1, 0)
            log_acc[...] += dot(rows, router_b[:, cols], 1, 1)

        chunks(body)
        ids = all_bwd[:, model:].astype(jnp.float32)
        one = (lane == ids[:, at : at + 1]).astype(jnp.float32)
        two = (lane == ids[:, at + 1 : at + 2]).astype(jnp.float32)
        logits = log_acc[...]
        apart = jnp.sum((one - two) * logits, axis=1, keepdims=True)
        first, second = jax.nn.sigmoid(apart), jax.nn.sigmoid(-apart)
        weight = jnp.sum((one * first + two * second) * mine, axis=1, keepdims=True)
        return one, two, first, second, weight, pre_acc[:, :width], pre_acc[:, width:]

    gather_bwd[0].start()
    normalize_into(saved, all_bwd, 1)
    gather_bwd[1].start()

    @pl.when(jnp.logical_not(has_next))
    def _():
        load_cot.wait()

    for h in range(2):
        @pl.when(has_next)
        def _():
            relay_grad(h).wait_recv()

        gather_up[h].start()
        gather_bwd[h].forward()

    @pl.when(has_prev)
    def _():
        for h in range(2):
            relay_out(h).wait_recv()

    @pl.when(jnp.logical_not(has_prev))
    def _():
        load_fresh.wait()

    normalize_into(inputs_fwd, all_fwd, 0)
    normalize_into(inputs_fwd, all_fwd, 1)
    load_gate.wait()
    load_down.wait()
    for h in range(2):
        gather_bwd[h].finish()
    one, two, first, second, weight, gate, up = project(all_bwd, 0)
    sig = jax.nn.sigmoid(gate)
    active = gate * sig
    hidden = active * up
    hid_weighted[...] = (weight * hidden).astype(jnp.bfloat16)

    gather_up[0].forward()
    gather_up[1].crossed()
    gather_fwd[0].start()
    gather_fwd[1].start()
    gather_up[1].pass_on()
    gather_up[0].finish()
    gather_up[1].finish()
    hid_acc[...] = jnp.zeros_like(hid_acc)

    def up_body(cols):
        hid_acc[...] += dot(all_up[:, cols], down_w[:, cols], 1, 1)

    chunks(up_body)
    up_down = hid_acc[...]
    gate_grad = jnp.sum(hidden * up_down, axis=1, keepdims=True)
    lanes = lax.broadcasted_iota(jnp.int32, (total, 128), 1).astype(jnp.float32)
    gates_all[me] = (gate_grad * (lanes == me.astype(jnp.float32)).astype(jnp.float32)).astype(
        jnp.bfloat16
    )
    gather_gate.start()
    hidden_grad = weight * up_down
    grad_pre[:, :width] = (hidden_grad * up * sig * (1.0 + gate * (1.0 - sig))).astype(jnp.bfloat16)
    grad_pre[:, width:] = (hidden_grad * active).astype(jnp.bfloat16)

    def gu_copy(i, k):
        return pltpu.make_async_remote_copy(
            src_ref=gu_send.at[i - 1, k], dst_ref=gu_recv.at[i - 1, k],
            send_sem=gu_ss.at[i - 1, k], recv_sem=gu_rs.at[i - 1, k],
            device_id={"dp": lax.rem(dp + i, replicas)}, device_id_type=MESH,
        )

    def dn_copy(i, k):
        return pltpu.make_async_remote_copy(
            src_ref=dn_send.at[i - 1, k], dst_ref=dn_recv.at[i - 1, k],
            send_sem=dn_ss.at[i - 1, k], recv_sem=dn_rs.at[i - 1, k],
            device_id={"dp": lax.rem(dp + i, replicas)}, device_id_type=MESH,
        )

    def weight_parts(owner, k):
        cols = pl.ds(pl.multiple_of(owner * piece + k * chunk, chunk), chunk)
        gu = dot(all_bwd[:, cols], grad_pre[...], 0, 0).astype(jnp.bfloat16)
        dn = dot(hid_weighted[...], all_up[:, cols], 0, 0).astype(jnp.bfloat16)
        return gu, dn

    for i in range(1, replicas):
        def send_step(k, carry, i=i):
            gu, dn = weight_parts(lax.rem(dp + i, replicas), k)
            gu_send[i - 1, k] = gu
            dn_send[i - 1, k] = dn
            gu_copy(i, k).start()
            dn_copy(i, k).start()
            return carry

        lax.fori_loop(0, steps, send_step, 0)

    def row_body(cols):
        part[:, cols] = dot(grad_pre[...], gate_up_w[cols, :], 1, 1).astype(jnp.bfloat16)

    chunks(row_body)
    scatter_row.start()

    def own_step(k, carry):
        gu, dn = weight_parts(dp, k)
        grad_gate_up[columns(k), :] = gu
        grad_down[:, columns(k)] = dn
        return carry

    gather_gate.forward()
    scatter_row.forward()
    lax.fori_loop(0, steps, own_step, 0)

    gather_gate.finish()
    gate_all = gates_all[0].astype(jnp.float32)
    for j in range(1, owners):
        gate_all = gate_all + gates_all[j].astype(jnp.float32)
    logit = (one - two) * (
        first * second * jnp.sum((one - two) * gate_all[:, :experts], axis=1, keepdims=True)
    )
    logit_ref[...] = logit

    def rt_copy(i):
        return pltpu.make_async_remote_copy(
            src_ref=rt_send.at[i - 1], dst_ref=rt_recv.at[i - 1],
            send_sem=rt_ss.at[i - 1], recv_sem=rt_rs.at[i - 1],
            device_id={"dp": lax.rem(dp + i, replicas)}, device_id_type=MESH,
        )

    def router_part(owner):
        cols = pl.ds(pl.multiple_of(owner * piece + me * rt_step, 128), rt_width)
        return dot(
            logit_ref[...], all_bwd[:, cols].astype(jnp.float32), 0, 0, lax.Precision.HIGHEST
        )

    for i in range(1, replicas):
        rt_send[i - 1] = router_part(lax.rem(dp + i, replicas))
        rt_copy(i).start()
    rt_own[...] = router_part(dp)

    gather_fwd[0].forward()
    gather_fwd[1].forward()
    for h in range(2):
        gather_fwd[h].finish()
        gather_bwd[h].sent()
    _, _, _, _, weight_f, gate_f, up_f = project(all_fwd, 2)
    hid_weighted[...] = (weight_f * (gate_f * jax.nn.sigmoid(gate_f) * up_f)).astype(jnp.bfloat16)

    def y_body(cols):
        all_bwd[:, cols] = dot(hid_weighted[...], down_w[:, cols], 1, 0).astype(jnp.bfloat16)

    chunks(y_body)
    scatter_y.start()
    scatter_y.forward()

    scatter_row.finish()

    def grad_body(at):
        rows = pl.ds(at, STRIP)
        home = pl.ds(pl.multiple_of(me * tokens + at, STRIP), STRIP)
        values = saved[rows, :].astype(jnp.float32)
        inv = inverse(values)
        unit = values * inv
        normed_grad = scatter_row.total(rows)
        steps_here = logit_ref[home, :]
        for j in range(experts):
            normed_grad = normed_grad + steps_here[:, j : j + 1] * router_b[j : j + 1, :].astype(
                jnp.float32
            )
        inner = jnp.mean(normed_grad * unit, axis=1, keepdims=True)
        input_grad[rows, :] = (
            all_up[home, :].astype(jnp.float32) + (normed_grad - unit * inner) * inv
        ).astype(jnp.bfloat16)

    strips(grad_body)

    rt = rt_own[...]
    for i in range(1, replicas):
        rt_copy(i).wait_recv()
        rt = rt + rt_recv[i - 1]
    grad_router[...] = rt

    for i in range(1, replicas):
        def add_step(k, carry, i=i):
            gu_copy(i, k).wait_recv()
            dn_copy(i, k).wait_recv()
            cols = columns(k)
            grad_gate_up[cols, :] = (
                grad_gate_up[cols, :].astype(jnp.float32) + gu_recv[i - 1, k].astype(jnp.float32)
            ).astype(jnp.bfloat16)
            grad_down[:, cols] = (
                grad_down[:, cols].astype(jnp.float32) + dn_recv[i - 1, k].astype(jnp.float32)
            ).astype(jnp.bfloat16)
            return carry

        lax.fori_loop(0, steps, add_step, 0)

    scatter_y.finish()

    def out_body(at):
        rows = pl.ds(at, STRIP)
        section_out[rows, :] = (
            inputs_fwd[rows, :].astype(jnp.float32) + scatter_y.total(rows)
        ).astype(jnp.bfloat16)

    strips(out_body)

    @pl.when(has_prev)
    def _():
        for h in range(2):
            relay_grad(h).wait_send()

    @pl.when(has_next)
    def _():
        for h in range(2):
            relay_out(h).wait_send()

    for h in range(2):
        gather_up[h].sent()
        gather_fwd[h].sent()
    gather_gate.sent()
    scatter_row.sent()
    scatter_y.sent()
    for i in range(1, replicas):
        rt_copy(i).wait_send()

        def drain(k, carry, i=i):
            gu_copy(i, k).wait_send()
            dn_copy(i, k).wait_send()
            return carry

        lax.fori_loop(0, steps, drain, 0)


def hand_over(*refs):
    count = (len(refs) - 1) // 2
    sems = refs[-1]
    copies = []
    for a in range(count):
        rows = refs[a].shape[0]
        parts = 2 if rows % 32 == 0 else 1
        for h in range(parts):
            at = pl.ds(h * (rows // parts), rows // parts)
            copies.append(
                pltpu.make_async_copy(refs[a].at[at], refs[count + a].at[at], sems.at[a, h])
            )
    for copy in copies:
        copy.start()
    for copy in copies:
        copy.wait()


def shards(
    fresh, cotangent, prev_out, prev_grad, saved_in, route_fwd, route_bwd, router, gate_up, down
):
    sections = lax.axis_size("pipe")
    replicas = lax.axis_size("dp")
    owners = lax.axis_size("expert")
    tokens, model = fresh.shape
    width = down.shape[2]
    experts = router.shape[2]
    chips = owners // 2
    total = owners * tokens
    piece = model // replicas
    chunk = min(768, piece)
    steps = piece // chunk
    rt_width = piece // owners if (piece // owners) % 128 == 0 else piece

    bf16, f32 = jnp.bfloat16, jnp.float32
    far = max(replicas - 1, 1)
    dma = pltpu.SemaphoreType.DMA
    hbm = pl.BlockSpec(memory_space=pltpu.HBM)
    vmem = pl.BlockSpec(memory_space=pltpu.VMEM)
    outs = pl.pallas_call(
        functools.partial(kernel, (sections, replicas, owners)),
        out_shape=(
            jax.ShapeDtypeStruct((tokens, model), bf16),
            jax.ShapeDtypeStruct((tokens, model), bf16),
            jax.ShapeDtypeStruct((piece, 2 * width), bf16),
            jax.ShapeDtypeStruct((width, piece), bf16),
            jax.ShapeDtypeStruct((experts, rt_width), f32),
        ),
        in_specs=[hbm] * 5 + [vmem] * 3 + [hbm] * 2,
        out_specs=(vmem,) * 5,
        scratch_shapes=[
            pltpu.VMEM((total, model + 128), bf16),
            pltpu.VMEM((total, model), bf16),
            pltpu.VMEM((total, model), bf16),
            pltpu.VMEM((total, model), bf16),
            pltpu.VMEM((chips, tokens, model), bf16),
            pltpu.VMEM((chips - 1, tokens, model), bf16),
            pltpu.VMEM((chips, tokens, model), bf16),
            pltpu.VMEM((chips - 1, tokens, model), bf16),
            pltpu.VMEM((model, 2 * width), bf16),
            pltpu.VMEM((width, model), bf16),
            pltpu.VMEM((tokens, model), bf16),
            pltpu.VMEM((tokens, model), bf16),
            pltpu.VMEM((far, steps, chunk, 2 * width), bf16),
            pltpu.VMEM((far, steps, chunk, 2 * width), bf16),
            pltpu.VMEM((far, steps, width, chunk), bf16),
            pltpu.VMEM((far, steps, width, chunk), bf16),
            pltpu.VMEM((far, experts, rt_width), f32),
            pltpu.VMEM((far, experts, rt_width), f32),
            pltpu.VMEM((owners, total, 128), bf16),
            pltpu.VMEM((total, 2 * width), f32),
            pltpu.VMEM((total, experts), f32),
            pltpu.VMEM((total, width), f32),
            pltpu.VMEM((total, 2 * width), bf16),
            pltpu.VMEM((total, width), bf16),
            pltpu.VMEM((total, experts), f32),
            pltpu.VMEM((experts, rt_width), f32),
            dma((5,)),
            dma((2, 2)),
            dma((2, 2)),
            dma((7, 2 * chips - 1)),
            dma((7, 2 * chips - 1)),
            dma((2, chips)),
            dma((2, chips)),
            dma((2, chips - 1)),
            dma((2, chips - 1)),
            dma((far, steps)),
            dma((far, steps)),
            dma((far, steps)),
            dma((far, steps)),
            dma((far,)),
            dma((far,)),
        ],
        compiler_params=pltpu.CompilerParams(
            collective_id=0, has_side_effects=True, vmem_limit_bytes=60 * 2**20
        ),
        name="relay_step",
    )(
        fresh, cotangent, prev_out[0], prev_grad[0], saved_in[0],
        route_bwd[0].T, route_fwd[0].T, router[0].T, gate_up[0, 0], down[0, 0],
    )
    section_out, input_grad, grad_gate_up, grad_down, grad_router = pl.pallas_call(
        hand_over,
        out_shape=[jax.ShapeDtypeStruct(out.shape, out.dtype) for out in outs],
        in_specs=[hbm] * 5,
        out_specs=[hbm] * 5,
        scratch_shapes=[dma((5, 2))],
        compiler_params=pltpu.CompilerParams(vmem_limit_bytes=60 * 2**20),
        name="hand_over",
    )(*outs)
    share = piece // owners
    if rt_width != share:
        grad_router = lax.dynamic_slice_in_dim(
            grad_router, lax.axis_index("expert") * share, share, axis=1
        )
    return (
        section_out[None],
        input_grad[None],
        grad_gate_up[None, None],
        grad_down[None, None],
        grad_router.T[None],
    )


def solution(mesh):
    tokens = P(("dp", "expert"), None)
    sectioned = P("pipe", ("dp", "expert"), None)
    return jax.shard_map(
        shards,
        mesh=mesh,
        in_specs=(
            tokens, tokens, sectioned, sectioned, sectioned, sectioned, sectioned,
            P("pipe", None, None),
            P("pipe", "expert", None, None),
            P("pipe", "expert", None, None),
        ),
        out_specs=(
            sectioned,
            sectioned,
            P("pipe", "expert", "dp", None),
            P("pipe", "expert", None, "dp"),
            sectioned,
        ),
        check_vma=False,
    )
```

```python
import functools

import jax
import jax.numpy as jnp
from jax import lax
from jax.experimental import pallas as pl
from jax.experimental.pallas import tpu as pltpu
from jax.sharding import PartitionSpec as P

EPSILON = 1e-05
MESH = pl.DeviceIdType.MESH
STRIP = 16


def dot(a, b, ca, cb, precision=None):
    return lax.dot_general(
        a, b, (((ca,), (cb,)), ((), ())), precision=precision, preferred_element_type=jnp.float32
    )


class Gather:
    def __init__(self, view, send, recv, chips, x, c):
        self.view, self.send, self.recv = view, send, recv
        self.chips, self.x, self.c = chips, x, c

    def copy(self, block, at, target):
        ref = self.view(block)
        return pltpu.make_async_remote_copy(
            src_ref=ref, dst_ref=ref, send_sem=self.send.at[at], recv_sem=self.recv.at[at],
            device_id={"expert": target}, device_id_type=MESH,
        )

    def here(self, i, core):
        return lax.rem(self.x + self.chips - i, self.chips) * 2 + core

    def start(self):
        own = self.x * 2 + self.c
        for i in range(1, self.chips):
            self.copy(own, i, lax.rem(self.x + i, self.chips) * 2 + self.c).start()
        self.copy(own, 0, self.x * 2 + 1 - self.c).start()

    def crossed(self):
        for i in range(1, self.chips):
            self.copy(self.here(i, self.c), i, self.x * 2 + 1 - self.c).wait_recv()

    def pass_on(self):
        other = self.x * 2 + 1 - self.c
        for i in range(1, self.chips):
            self.copy(self.here(i, self.c), self.chips - 1 + i, other).start()

    def forward(self):
        self.crossed()
        self.pass_on()

    def finish(self):
        other = self.x * 2 + 1 - self.c
        self.copy(other, 0, other).wait_recv()
        for i in range(1, self.chips):
            self.copy(self.here(i, 1 - self.c), self.chips - 1 + i, other).wait_recv()

    def sent(self):
        other = self.x * 2 + 1 - self.c
        own = self.x * 2 + self.c
        self.copy(own, 0, other).wait_send()
        for i in range(1, self.chips):
            self.copy(own, i, other).wait_send()
            self.copy(self.here(i, self.c), self.chips - 1 + i, other).wait_send()


class Scatter:
    def __init__(self, view, pair, cross, sems, chips, x, c):
        self.view, self.pair, self.cross = view, pair, cross
        self.pair_send, self.pair_recv, self.cross_send, self.cross_recv = sems
        self.chips, self.x, self.c = chips, x, c

    def pair_copy(self, i):
        to = lax.rem(self.x + i, self.chips) * 2 + 1 - self.c
        return pltpu.make_async_remote_copy(
            src_ref=self.view(to), dst_ref=self.pair.at[i],
            send_sem=self.pair_send.at[i], recv_sem=self.pair_recv.at[i],
            device_id={"expert": self.x * 2 + 1 - self.c}, device_id_type=MESH,
        )

    def cross_copy(self, i):
        return pltpu.make_async_remote_copy(
            src_ref=self.pair.at[i], dst_ref=self.cross.at[i - 1],
            send_sem=self.cross_send.at[i - 1], recv_sem=self.cross_recv.at[i - 1],
            device_id={"expert": lax.rem(self.x + i, self.chips) * 2 + self.c}, device_id_type=MESH,
        )

    def order(self):
        return list(range(1, self.chips)) + [0]

    def start(self):
        for i in self.order():
            self.pair_copy(i).start()

    def forward(self):
        for i in range(1, self.chips):
            self.pair_copy(i).wait_recv()
            mine = self.view(lax.rem(self.x + i, self.chips) * 2 + self.c)

            def add(k, carry, i=i, mine=mine):
                rows = pl.ds(pl.multiple_of(k * STRIP, STRIP), STRIP)
                self.pair[i, rows, :] = (
                    self.pair[i, rows, :].astype(jnp.float32) + mine[rows, :].astype(jnp.float32)
                ).astype(jnp.bfloat16)
                return carry

            lax.fori_loop(0, self.pair.shape[1] // STRIP, add, 0)
            self.cross_copy(i).start()

    def finish(self):
        self.pair_copy(0).wait_recv()
        for i in range(1, self.chips):
            self.cross_copy(i).wait_recv()

    def total(self, rows):
        value = self.view(self.x * 2 + self.c)[rows, :].astype(jnp.float32)
        value = value + self.pair[0, rows, :].astype(jnp.float32)
        for i in range(1, self.chips):
            value = value + self.cross[i - 1, rows, :].astype(jnp.float32)
        return value

    def sent(self):
        for i in range(self.chips):
            self.pair_copy(i).wait_send()
        for i in range(1, self.chips):
            self.cross_copy(i).wait_send()


def kernel(
    dims,
    fresh, cotangent, prev_out, prev_grad, saved_in, ids_bwd, ids_fwd, router_b,
    gate_up, down,
    section_out, input_grad, grad_gate_up, grad_down, grad_router,
    all_bwd, all_fwd, all_up, part, pair_row, cross_row, pair_y, cross_y,
    gate_up_w, down_w, saved, inputs_fwd, gu_send, gu_recv, dn_send, dn_recv, rt_send, rt_recv,
    gates_all, pre_acc, log_acc, hid_acc, grad_pre, hid_weighted, logit_ref, rt_own,
    local_sem, pipe_send, pipe_recv, g_send, g_recv, s_psend, s_precv, s_csend, s_crecv,
    gu_ss, gu_rs, dn_ss, dn_rs, rt_ss, rt_rs,
):
    sections, replicas, owners = dims
    tokens, model = saved.shape
    width = down_w.shape[0]
    experts = router_b.shape[0]
    half = tokens // 2
    chips = owners // 2
    total = owners * tokens
    piece = model // replicas
    chunk = gu_send.shape[2]
    steps = gu_send.shape[1]
    rt_width = rt_own.shape[1]
    rt_step = rt_width if rt_width < piece else 0

    section = lax.axis_index("pipe")
    dp = lax.axis_index("dp")
    me = lax.axis_index("expert")
    x, c = me // 2, lax.rem(me, 2)
    has_prev = section > 0
    has_next = section < sections - 1
    own_rows = pl.ds(pl.multiple_of(me * tokens, tokens), tokens)

    load_saved = pltpu.make_async_copy(saved_in, saved, local_sem.at[0])
    load_gate = pltpu.make_async_copy(gate_up, gate_up_w, local_sem.at[1])
    load_down = pltpu.make_async_copy(down, down_w, local_sem.at[2])
    load_fresh = pltpu.make_async_copy(fresh, inputs_fwd, local_sem.at[3])
    load_cot = pltpu.make_async_copy(cotangent, all_up.at[own_rows], local_sem.at[4])
    load_saved.start()
    load_gate.start()
    load_down.start()

    barrier = pltpu.get_barrier_semaphore()

    @pl.when(has_prev)
    def _():
        pl.semaphore_signal(barrier, inc=1, device_id={"pipe": section - 1}, device_id_type=MESH)

    @pl.when(has_next)
    def _():
        pl.semaphore_signal(barrier, inc=1, device_id={"pipe": section + 1}, device_id_type=MESH)

    pl.semaphore_signal(barrier, inc=1, device_id={"expert": x * 2 + 1 - c}, device_id_type=MESH)
    for i in range(1, chips):
        pl.semaphore_signal(
            barrier, inc=1, device_id={"expert": lax.rem(x + i, chips) * 2 + c}, device_id_type=MESH
        )
    for i in range(1, replicas):
        pl.semaphore_signal(
            barrier, inc=1, device_id={"dp": lax.rem(dp + i, replicas)}, device_id_type=MESH
        )

    def strips(body):
        def step(k, carry):
            body(pl.multiple_of(k * STRIP, STRIP))
            return carry

        lax.fori_loop(0, tokens // STRIP, step, 0)

    def inverse(values):
        return 1.0 / jnp.sqrt(jnp.mean(values * values, axis=1, keepdims=True) + EPSILON)

    def normalize_into(source, target, part_at):
        def step(k, carry):
            at = pl.multiple_of(part_at * half + k * STRIP, STRIP)
            values = source[pl.ds(at, STRIP), :].astype(jnp.float32)
            rows = pl.ds(pl.multiple_of(me * tokens + at, STRIP), STRIP)
            target[rows, :model] = (values * inverse(values)).astype(jnp.bfloat16)
            return carry

        lax.fori_loop(0, half // STRIP, step, 0)

    load_saved.wait()
    spot = lax.broadcasted_iota(jnp.int32, (2, 128), 0)
    slot = lax.broadcasted_iota(jnp.int32, (2, 128), 1)
    all_bwd[own_rows, model:] = (
        dot(ids_bwd[...].astype(jnp.float32), (slot == spot).astype(jnp.float32), 0, 0)
        + dot(ids_fwd[...].astype(jnp.float32), (slot == spot + 2).astype(jnp.float32), 0, 0)
    ).astype(jnp.bfloat16)
    normalize_into(saved, all_bwd, 0)
    pl.semaphore_wait(
        barrier,
        chips + replicas - 1 + jnp.minimum(section, 1) + jnp.minimum(sections - 1 - section, 1),
    )

    def relay_out(h):
        rows = pl.ds(h * half, half)
        return pltpu.make_async_remote_copy(
            src_ref=prev_out.at[rows], dst_ref=inputs_fwd.at[rows],
            send_sem=pipe_send.at[0, h], recv_sem=pipe_recv.at[0, h],
            device_id={"pipe": lax.rem(section + 1, sections)}, device_id_type=MESH,
        )

    def relay_grad(h):
        cols = pl.ds(h * (model // 2), model // 2)
        return pltpu.make_async_remote_copy(
            src_ref=prev_grad.at[:, cols], dst_ref=all_up.at[own_rows, cols],
            send_sem=pipe_send.at[1, h], recv_sem=pipe_recv.at[1, h],
            device_id={"pipe": lax.rem(section + sections - 1, sections)}, device_id_type=MESH,
        )

    @pl.when(has_prev)
    def _():
        for h in range(2):
            relay_grad(h).start()

    @pl.when(has_next)
    def _():
        for h in range(2):
            relay_out(h).start()

    @pl.when(jnp.logical_not(has_prev))
    def _():
        load_fresh.start()

    @pl.when(jnp.logical_not(has_next))
    def _():
        load_cot.start()

    def block_of(ref):
        return lambda j: ref.at[pl.ds(pl.multiple_of(j * tokens, tokens), tokens)]

    def halves(ref, a):
        def view(h):
            return lambda j: ref.at[pl.ds(pl.multiple_of(j * tokens + h * half, half), half)]

        return [
            Gather(view(h), g_send.at[2 * a + h], g_recv.at[2 * a + h], chips, x, c)
            for h in range(2)
        ]

    def column_halves(ref, a):
        def view(h):
            cols = pl.ds(h * (model // 2), model // 2)
            return lambda j: ref.at[pl.ds(pl.multiple_of(j * tokens, tokens), tokens), cols]

        return [
            Gather(view(h), g_send.at[2 * a + h], g_recv.at[2 * a + h], chips, x, c)
            for h in range(2)
        ]

    gather_bwd = halves(all_bwd, 0)
    gather_up = column_halves(all_up, 1)
    gather_fwd = column_halves(all_fwd, 2)
    gather_gate = Gather(lambda j: gates_all.at[j], g_send.at[6], g_recv.at[6], chips, x, c)
    sems = [
        tuple(ref.at[a] for ref in (s_psend, s_precv, s_csend, s_crecv)) for a in range(2)
    ]
    scatter_row = Scatter(block_of(part), pair_row, cross_row, sems[0], chips, x, c)

    def narrow(j):
        return all_bwd.at[pl.ds(pl.multiple_of(j * tokens, tokens), tokens), pl.ds(0, model)]

    scatter_y = Scatter(narrow, pair_y, cross_y, sems[1], chips, x, c)

    def columns(k):
        return pl.ds(pl.multiple_of(k * chunk, chunk), chunk)

    every = model // chunk

    def chunks(body, begin=0, end=every):
        def step(k, carry):
            body(columns(k))
            return carry

        lax.fori_loop(begin, end, step, 0)

    lane = lax.broadcasted_iota(jnp.int32, (total, experts), 1).astype(jnp.float32)
    mine = (lane == me.astype(jnp.float32)).astype(jnp.float32)

    def project(rows_ref, at, ready):
        pre_acc[...] = jnp.zeros_like(pre_acc)
        log_acc[...] = jnp.zeros_like(log_acc)

        def body(cols):
            rows = rows_ref[:, cols]
            pre_acc[...] += dot(rows, gate_up_w[cols, :], 1, 0)
            log_acc[...] += dot(rows, router_b[:, cols], 1, 1)

        for h in range(2):
            ready(h)
            chunks(body, h * every // 2, (h + 1) * every // 2)
        ids = all_bwd[:, model:].astype(jnp.float32)
        one = (lane == ids[:, at : at + 1]).astype(jnp.float32)
        two = (lane == ids[:, at + 1 : at + 2]).astype(jnp.float32)
        logits = log_acc[...]
        apart = jnp.sum((one - two) * logits, axis=1, keepdims=True)
        first, second = jax.nn.sigmoid(apart), jax.nn.sigmoid(-apart)
        weight = jnp.sum((one * first + two * second) * mine, axis=1, keepdims=True)
        return one, two, first, second, weight, pre_acc[:, :width], pre_acc[:, width:]

    gather_bwd[0].start()
    normalize_into(saved, all_bwd, 1)
    gather_bwd[1].start()

    @pl.when(jnp.logical_not(has_next))
    def _():
        load_cot.wait()

    for h in range(2):
        @pl.when(has_next)
        def _():
            relay_grad(h).wait_recv()

        gather_up[h].start()
        gather_bwd[h].forward()

    @pl.when(has_prev)
    def _():
        for h in range(2):
            relay_out(h).wait_recv()

    @pl.when(jnp.logical_not(has_prev))
    def _():
        load_fresh.wait()

    normalize_into(inputs_fwd, all_fwd, 0)
    normalize_into(inputs_fwd, all_fwd, 1)
    load_gate.wait()
    load_down.wait()
    for h in range(2):
        gather_bwd[h].finish()
    one, two, first, second, weight, gate, up = project(all_bwd, 0, lambda h: None)
    sig = jax.nn.sigmoid(gate)
    active = gate * sig
    hidden = active * up
    hid_weighted[...] = (weight * hidden).astype(jnp.bfloat16)

    gather_up[0].forward()
    gather_up[1].crossed()
    gather_fwd[0].start()
    gather_fwd[1].start()
    gather_up[1].pass_on()
    hid_acc[...] = jnp.zeros_like(hid_acc)

    def up_body(cols):
        hid_acc[...] += dot(all_up[:, cols], down_w[:, cols], 1, 1)

    for h in range(2):
        gather_up[h].finish()
        chunks(up_body, h * every // 2, (h + 1) * every // 2)
    up_down = hid_acc[...]
    gate_grad = jnp.sum(hidden * up_down, axis=1, keepdims=True)
    lanes = lax.broadcasted_iota(jnp.int32, (total, 128), 1).astype(jnp.float32)
    gates_all[me] = (gate_grad * (lanes == me.astype(jnp.float32)).astype(jnp.float32)).astype(
        jnp.bfloat16
    )
    gather_gate.start()
    hidden_grad = weight * up_down
    grad_pre[:, :width] = (hidden_grad * up * sig * (1.0 + gate * (1.0 - sig))).astype(jnp.bfloat16)
    grad_pre[:, width:] = (hidden_grad * active).astype(jnp.bfloat16)

    def gu_copy(i, k):
        return pltpu.make_async_remote_copy(
            src_ref=gu_send.at[i - 1, k], dst_ref=gu_recv.at[i - 1, k],
            send_sem=gu_ss.at[i - 1, k], recv_sem=gu_rs.at[i - 1, k],
            device_id={"dp": lax.rem(dp + i, replicas)}, device_id_type=MESH,
        )

    def dn_copy(i, k):
        return pltpu.make_async_remote_copy(
            src_ref=dn_send.at[i - 1, k], dst_ref=dn_recv.at[i - 1, k],
            send_sem=dn_ss.at[i - 1, k], recv_sem=dn_rs.at[i - 1, k],
            device_id={"dp": lax.rem(dp + i, replicas)}, device_id_type=MESH,
        )

    def weight_parts(owner, k):
        cols = pl.ds(pl.multiple_of(owner * piece + k * chunk, chunk), chunk)
        gu = dot(all_bwd[:, cols], grad_pre[...], 0, 0).astype(jnp.bfloat16)
        dn = dot(hid_weighted[...], all_up[:, cols], 0, 0).astype(jnp.bfloat16)
        return gu, dn

    for i in range(1, replicas):
        def send_step(k, carry, i=i):
            gu, dn = weight_parts(lax.rem(dp + i, replicas), k)
            gu_send[i - 1, k] = gu
            dn_send[i - 1, k] = dn
            gu_copy(i, k).start()
            dn_copy(i, k).start()
            return carry

        lax.fori_loop(0, steps, send_step, 0)

    def row_body(cols):
        part[:, cols] = dot(grad_pre[...], gate_up_w[cols, :], 1, 1).astype(jnp.bfloat16)

    chunks(row_body)
    scatter_row.start()

    def own_step(k, carry):
        gu, dn = weight_parts(dp, k)
        grad_gate_up[columns(k), :] = gu
        grad_down[:, columns(k)] = dn
        return carry

    gather_gate.forward()
    scatter_row.forward()
    lax.fori_loop(0, steps, own_step, 0)

    gather_gate.finish()
    gate_all = gates_all[0].astype(jnp.float32)
    for j in range(1, owners):
        gate_all = gate_all + gates_all[j].astype(jnp.float32)
    logit = (one - two) * (
        first * second * jnp.sum((one - two) * gate_all[:, :experts], axis=1, keepdims=True)
    )
    logit_ref[...] = logit

    def rt_copy(i):
        return pltpu.make_async_remote_copy(
            src_ref=rt_send.at[i - 1], dst_ref=rt_recv.at[i - 1],
            send_sem=rt_ss.at[i - 1], recv_sem=rt_rs.at[i - 1],
            device_id={"dp": lax.rem(dp + i, replicas)}, device_id_type=MESH,
        )

    def router_part(owner):
        cols = pl.ds(pl.multiple_of(owner * piece + me * rt_step, 128), rt_width)
        return dot(
            logit_ref[...], all_bwd[:, cols].astype(jnp.float32), 0, 0, lax.Precision.HIGHEST
        )

    for i in range(1, replicas):
        rt_send[i - 1] = router_part(lax.rem(dp + i, replicas))
        rt_copy(i).start()
    rt_own[...] = router_part(dp)

    def fwd_ready(h):
        gather_fwd[h].forward()
        gather_fwd[h].finish()

    for h in range(2):
        gather_bwd[h].sent()
    _, _, _, _, weight_f, gate_f, up_f = project(all_fwd, 2, fwd_ready)
    hid_weighted[...] = (weight_f * (gate_f * jax.nn.sigmoid(gate_f) * up_f)).astype(jnp.bfloat16)

    def y_body(cols):
        all_bwd[:, cols] = dot(hid_weighted[...], down_w[:, cols], 1, 0).astype(jnp.bfloat16)

    chunks(y_body)
    scatter_y.start()
    scatter_y.forward()

    scatter_row.finish()

    def grad_body(at):
        rows = pl.ds(at, STRIP)
        home = pl.ds(pl.multiple_of(me * tokens + at, STRIP), STRIP)
        values = saved[rows, :].astype(jnp.float32)
        inv = inverse(values)
        unit = values * inv
        normed_grad = scatter_row.total(rows)
        steps_here = logit_ref[home, :]
        for j in range(experts):
            normed_grad = normed_grad + steps_here[:, j : j + 1] * router_b[j : j + 1, :].astype(
                jnp.float32
            )
        inner = jnp.mean(normed_grad * unit, axis=1, keepdims=True)
        input_grad[rows, :] = (
            all_up[home, :].astype(jnp.float32) + (normed_grad - unit * inner) * inv
        ).astype(jnp.bfloat16)

    strips(grad_body)

    rt = rt_own[...]
    for i in range(1, replicas):
        rt_copy(i).wait_recv()
        rt = rt + rt_recv[i - 1]
    grad_router[...] = rt

    for i in range(1, replicas):
        def add_step(k, carry, i=i):
            gu_copy(i, k).wait_recv()
            dn_copy(i, k).wait_recv()
            cols = columns(k)
            grad_gate_up[cols, :] = (
                grad_gate_up[cols, :].astype(jnp.float32) + gu_recv[i - 1, k].astype(jnp.float32)
            ).astype(jnp.bfloat16)
            grad_down[:, cols] = (
                grad_down[:, cols].astype(jnp.float32) + dn_recv[i - 1, k].astype(jnp.float32)
            ).astype(jnp.bfloat16)
            return carry

        lax.fori_loop(0, steps, add_step, 0)

    scatter_y.finish()

    def out_body(at):
        rows = pl.ds(at, STRIP)
        section_out[rows, :] = (
            inputs_fwd[rows, :].astype(jnp.float32) + scatter_y.total(rows)
        ).astype(jnp.bfloat16)

    strips(out_body)

    @pl.when(has_prev)
    def _():
        for h in range(2):
            relay_grad(h).wait_send()

    @pl.when(has_next)
    def _():
        for h in range(2):
            relay_out(h).wait_send()

    for h in range(2):
        gather_up[h].sent()
        gather_fwd[h].sent()
    gather_gate.sent()
    scatter_row.sent()
    scatter_y.sent()
    for i in range(1, replicas):
        rt_copy(i).wait_send()

        def drain(k, carry, i=i):
            gu_copy(i, k).wait_send()
            dn_copy(i, k).wait_send()
            return carry

        lax.fori_loop(0, steps, drain, 0)


def hand_over(*refs):
    sources, targets, stages, arrive, leave = refs[:5], refs[5:10], refs[10:15], refs[15], refs[16]
    copies = []
    for a in range(5):
        rows = sources[a].shape[0]
        parts = 2 if rows % 32 == 0 else 1
        for h in range(parts):
            at = pl.ds(h * (rows // parts), rows // parts)
            copies.append(
                (
                    pltpu.make_async_copy(sources[a].at[at], stages[a].at[at], arrive.at[a, h]),
                    pltpu.make_async_copy(stages[a].at[at], targets[a].at[at], leave.at[a, h]),
                )
            )
    for first, _ in copies:
        first.start()
    for first, then in copies:
        first.wait()
        then.start()
    for _, then in copies:
        then.wait()


def shards(
    fresh, cotangent, prev_out, prev_grad, saved_in, route_fwd, route_bwd, router, gate_up, down
):
    sections = lax.axis_size("pipe")
    replicas = lax.axis_size("dp")
    owners = lax.axis_size("expert")
    tokens, model = fresh.shape
    width = down.shape[2]
    experts = router.shape[2]
    chips = owners // 2
    total = owners * tokens
    piece = model // replicas
    chunk = min(768, piece)
    steps = piece // chunk
    rt_width = piece // owners if (piece // owners) % 128 == 0 else piece

    bf16, f32 = jnp.bfloat16, jnp.float32
    far = max(replicas - 1, 1)
    dma = pltpu.SemaphoreType.DMA
    hbm = pl.BlockSpec(memory_space=pltpu.HBM)
    vmem = pl.BlockSpec(memory_space=pltpu.VMEM)
    outs = pl.pallas_call(
        functools.partial(kernel, (sections, replicas, owners)),
        out_shape=(
            jax.ShapeDtypeStruct((tokens, model), bf16),
            jax.ShapeDtypeStruct((tokens, model), bf16),
            jax.ShapeDtypeStruct((piece, 2 * width), bf16),
            jax.ShapeDtypeStruct((width, piece), bf16),
            jax.ShapeDtypeStruct((experts, rt_width), f32),
        ),
        in_specs=[hbm] * 5 + [vmem] * 3 + [hbm] * 2,
        out_specs=(vmem,) * 5,
        scratch_shapes=[
            pltpu.VMEM((total, model + 128), bf16),
            pltpu.VMEM((total, model), bf16),
            pltpu.VMEM((total, model), bf16),
            pltpu.VMEM((total, model), bf16),
            pltpu.VMEM((chips, tokens, model), bf16),
            pltpu.VMEM((chips - 1, tokens, model), bf16),
            pltpu.VMEM((chips, tokens, model), bf16),
            pltpu.VMEM((chips - 1, tokens, model), bf16),
            pltpu.VMEM((model, 2 * width), bf16),
            pltpu.VMEM((width, model), bf16),
            pltpu.VMEM((tokens, model), bf16),
            pltpu.VMEM((tokens, model), bf16),
            pltpu.VMEM((far, steps, chunk, 2 * width), bf16),
            pltpu.VMEM((far, steps, chunk, 2 * width), bf16),
            pltpu.VMEM((far, steps, width, chunk), bf16),
            pltpu.VMEM((far, steps, width, chunk), bf16),
            pltpu.VMEM((far, experts, rt_width), f32),
            pltpu.VMEM((far, experts, rt_width), f32),
            pltpu.VMEM((owners, total, 128), bf16),
            pltpu.VMEM((total, 2 * width), f32),
            pltpu.VMEM((total, experts), f32),
            pltpu.VMEM((total, width), f32),
            pltpu.VMEM((total, 2 * width), bf16),
            pltpu.VMEM((total, width), bf16),
            pltpu.VMEM((total, experts), f32),
            pltpu.VMEM((experts, rt_width), f32),
            dma((5,)),
            dma((2, 2)),
            dma((2, 2)),
            dma((7, 2 * chips - 1)),
            dma((7, 2 * chips - 1)),
            dma((2, chips)),
            dma((2, chips)),
            dma((2, chips - 1)),
            dma((2, chips - 1)),
            dma((far, steps)),
            dma((far, steps)),
            dma((far, steps)),
            dma((far, steps)),
            dma((far,)),
            dma((far,)),
        ],
        compiler_params=pltpu.CompilerParams(
            collective_id=0, has_side_effects=True, vmem_limit_bytes=60 * 2**20
        ),
        name="relay_step",
    )(
        fresh, cotangent, prev_out[0], prev_grad[0], saved_in[0],
        route_bwd[0].T, route_fwd[0].T, router[0].T, gate_up[0, 0], down[0, 0],
    )
    section_out, input_grad, grad_gate_up, grad_down, grad_router = pl.pallas_call(
        hand_over,
        out_shape=[jax.ShapeDtypeStruct(out.shape, out.dtype) for out in outs],
        in_specs=[hbm] * 5,
        out_specs=[hbm] * 5,
        scratch_shapes=[pltpu.VMEM(out.shape, out.dtype) for out in outs]
        + [dma((5, 2)), dma((5, 2))],
        compiler_params=pltpu.CompilerParams(vmem_limit_bytes=60 * 2**20),
        name="hand_over",
    )(*outs)
    share = piece // owners
    if rt_width != share:
        grad_router = lax.dynamic_slice_in_dim(
            grad_router, lax.axis_index("expert") * share, share, axis=1
        )
    return (
        section_out[None],
        input_grad[None],
        grad_gate_up[None, None],
        grad_down[None, None],
        grad_router.T[None],
    )


def solution(mesh):
    tokens = P(("dp", "expert"), None)
    sectioned = P("pipe", ("dp", "expert"), None)
    return jax.shard_map(
        shards,
        mesh=mesh,
        in_specs=(
            tokens, tokens, sectioned, sectioned, sectioned, sectioned, sectioned,
            P("pipe", None, None),
            P("pipe", "expert", None, None),
            P("pipe", "expert", None, None),
        ),
        out_specs=(
            sectioned,
            sectioned,
            P("pipe", "expert", "dp", None),
            P("pipe", "expert", None, "dp"),
            sectioned,
        ),
        check_vma=False,
    )
```

```python
import functools

import jax
import jax.numpy as jnp
from jax import lax
from jax.experimental import pallas as pl
from jax.experimental.pallas import tpu as pltpu
from jax.sharding import PartitionSpec as P

EPSILON = 1e-05
MESH = pl.DeviceIdType.MESH
STRIP = 16


def dot(a, b, ca, cb, precision=None):
    return lax.dot_general(
        a, b, (((ca,), (cb,)), ((), ())), precision=precision, preferred_element_type=jnp.float32
    )


class Gather:
    def __init__(self, view, send, recv, chips, x, c):
        self.view, self.send, self.recv = view, send, recv
        self.chips, self.x, self.c = chips, x, c

    def copy(self, block, at, target):
        ref = self.view(block)
        return pltpu.make_async_remote_copy(
            src_ref=ref, dst_ref=ref, send_sem=self.send.at[at], recv_sem=self.recv.at[at],
            device_id={"expert": target}, device_id_type=MESH,
        )

    def here(self, i, core):
        return lax.rem(self.x + self.chips - i, self.chips) * 2 + core

    def start(self):
        own = self.x * 2 + self.c
        for i in range(1, self.chips):
            self.copy(own, i, lax.rem(self.x + i, self.chips) * 2 + self.c).start()
        self.copy(own, 0, self.x * 2 + 1 - self.c).start()

    def crossed(self):
        for i in range(1, self.chips):
            self.copy(self.here(i, self.c), i, self.x * 2 + 1 - self.c).wait_recv()

    def pass_on(self):
        other = self.x * 2 + 1 - self.c
        for i in range(1, self.chips):
            self.copy(self.here(i, self.c), self.chips - 1 + i, other).start()

    def forward(self):
        self.crossed()
        self.pass_on()

    def finish(self):
        other = self.x * 2 + 1 - self.c
        self.copy(other, 0, other).wait_recv()
        for i in range(1, self.chips):
            self.copy(self.here(i, 1 - self.c), self.chips - 1 + i, other).wait_recv()

    def sent(self):
        other = self.x * 2 + 1 - self.c
        own = self.x * 2 + self.c
        self.copy(own, 0, other).wait_send()
        for i in range(1, self.chips):
            self.copy(own, i, other).wait_send()
            self.copy(self.here(i, self.c), self.chips - 1 + i, other).wait_send()


class Scatter:
    def __init__(self, view, pair, cross, sems, chips, x, c):
        self.view, self.pair, self.cross = view, pair, cross
        self.pair_send, self.pair_recv, self.cross_send, self.cross_recv = sems
        self.chips, self.x, self.c = chips, x, c

    def pair_copy(self, i):
        to = lax.rem(self.x + i, self.chips) * 2 + 1 - self.c
        return pltpu.make_async_remote_copy(
            src_ref=self.view(to), dst_ref=self.pair.at[i],
            send_sem=self.pair_send.at[i], recv_sem=self.pair_recv.at[i],
            device_id={"expert": self.x * 2 + 1 - self.c}, device_id_type=MESH,
        )

    def cross_copy(self, i):
        return pltpu.make_async_remote_copy(
            src_ref=self.pair.at[i], dst_ref=self.cross.at[i - 1],
            send_sem=self.cross_send.at[i - 1], recv_sem=self.cross_recv.at[i - 1],
            device_id={"expert": lax.rem(self.x + i, self.chips) * 2 + self.c}, device_id_type=MESH,
        )

    def order(self):
        return list(range(1, self.chips)) + [0]

    def start(self):
        for i in self.order():
            self.pair_copy(i).start()

    def forward(self):
        for i in range(1, self.chips):
            self.pair_copy(i).wait_recv()
            mine = self.view(lax.rem(self.x + i, self.chips) * 2 + self.c)

            def add(k, carry, i=i, mine=mine):
                rows = pl.ds(pl.multiple_of(k * STRIP, STRIP), STRIP)
                self.pair[i, rows, :] = (
                    self.pair[i, rows, :].astype(jnp.float32) + mine[rows, :].astype(jnp.float32)
                ).astype(jnp.bfloat16)
                return carry

            lax.fori_loop(0, self.pair.shape[1] // STRIP, add, 0)
            self.cross_copy(i).start()

    def finish(self):
        self.pair_copy(0).wait_recv()
        for i in range(1, self.chips):
            self.cross_copy(i).wait_recv()

    def total(self, rows):
        value = self.view(self.x * 2 + self.c)[rows, :].astype(jnp.float32)
        value = value + self.pair[0, rows, :].astype(jnp.float32)
        for i in range(1, self.chips):
            value = value + self.cross[i - 1, rows, :].astype(jnp.float32)
        return value

    def sent(self):
        for i in range(self.chips):
            self.pair_copy(i).wait_send()
        for i in range(1, self.chips):
            self.cross_copy(i).wait_send()


def kernel(
    dims,
    fresh, cotangent, prev_out, prev_grad, saved_in, ids_bwd, ids_fwd, router_b,
    gate_up, down,
    section_out, input_grad, grad_gate_up, grad_down, grad_router,
    all_bwd, all_fwd, all_up, part, pair_row, cross_row, pair_y, cross_y,
    gate_up_w, down_w, saved, inputs_fwd, gu_send, gu_recv, dn_send, dn_recv, rt_send, rt_recv,
    gates_all, pre_acc, log_acc, hid_acc, grad_pre, hid_weighted, logit_ref, rt_own,
    local_sem, pipe_send, pipe_recv, g_send, g_recv, s_psend, s_precv, s_csend, s_crecv,
    gu_ss, gu_rs, dn_ss, dn_rs, rt_ss, rt_rs,
):
    sections, replicas, owners = dims
    tokens, model = saved.shape
    width = down_w.shape[0]
    experts = router_b.shape[0]
    half = tokens // 2
    chips = owners // 2
    total = owners * tokens
    piece = model // replicas
    chunk = gu_send.shape[2]
    steps = gu_send.shape[1]
    rt_width = rt_own.shape[1]
    rt_step = rt_width if rt_width < piece else 0

    section = lax.axis_index("pipe")
    dp = lax.axis_index("dp")
    me = lax.axis_index("expert")
    x, c = me // 2, lax.rem(me, 2)
    has_prev = section > 0
    has_next = section < sections - 1
    own_rows = pl.ds(pl.multiple_of(me * tokens, tokens), tokens)

    load_saved = pltpu.make_async_copy(saved_in, saved, local_sem.at[0])
    load_gate = pltpu.make_async_copy(gate_up, gate_up_w, local_sem.at[1])
    load_down = pltpu.make_async_copy(down, down_w, local_sem.at[2])
    load_fresh = pltpu.make_async_copy(fresh, inputs_fwd, local_sem.at[3])
    load_cot = pltpu.make_async_copy(cotangent, all_up.at[own_rows], local_sem.at[4])
    load_saved.start()
    load_gate.start()
    load_down.start()

    barrier = pltpu.get_barrier_semaphore()

    @pl.when(has_prev)
    def _():
        pl.semaphore_signal(barrier, inc=1, device_id={"pipe": section - 1}, device_id_type=MESH)

    @pl.when(has_next)
    def _():
        pl.semaphore_signal(barrier, inc=1, device_id={"pipe": section + 1}, device_id_type=MESH)

    pl.semaphore_signal(barrier, inc=1, device_id={"expert": x * 2 + 1 - c}, device_id_type=MESH)
    for i in range(1, chips):
        pl.semaphore_signal(
            barrier, inc=1, device_id={"expert": lax.rem(x + i, chips) * 2 + c}, device_id_type=MESH
        )
    for i in range(1, replicas):
        pl.semaphore_signal(
            barrier, inc=1, device_id={"dp": lax.rem(dp + i, replicas)}, device_id_type=MESH
        )

    def strips(body):
        def step(k, carry):
            body(pl.multiple_of(k * STRIP, STRIP))
            return carry

        lax.fori_loop(0, tokens // STRIP, step, 0)

    def inverse(values):
        return 1.0 / jnp.sqrt(jnp.mean(values * values, axis=1, keepdims=True) + EPSILON)

    def normalize_into(source, target, part_at):
        def step(k, carry):
            at = pl.multiple_of(part_at * half + k * STRIP, STRIP)
            values = source[pl.ds(at, STRIP), :].astype(jnp.float32)
            rows = pl.ds(pl.multiple_of(me * tokens + at, STRIP), STRIP)
            target[rows, :model] = (values * inverse(values)).astype(jnp.bfloat16)
            return carry

        lax.fori_loop(0, half // STRIP, step, 0)

    load_saved.wait()
    spot = lax.broadcasted_iota(jnp.int32, (2, 128), 0)
    slot = lax.broadcasted_iota(jnp.int32, (2, 128), 1)
    all_bwd[own_rows, model:] = (
        dot(ids_bwd[...].astype(jnp.float32), (slot == spot).astype(jnp.float32), 0, 0)
        + dot(ids_fwd[...].astype(jnp.float32), (slot == spot + 2).astype(jnp.float32), 0, 0)
    ).astype(jnp.bfloat16)
    normalize_into(saved, all_bwd, 0)
    pl.semaphore_wait(
        barrier,
        chips + replicas - 1 + jnp.minimum(section, 1) + jnp.minimum(sections - 1 - section, 1),
    )

    def up_half(h):
        return lax.rem(dp + 1 + h, 2) if replicas == 2 else h

    def up_columns(h):
        return pl.ds(pl.multiple_of(up_half(h) * (model // 2), model // 2), model // 2)

    def relay_out(h):
        rows = pl.ds(h * half, half)
        return pltpu.make_async_remote_copy(
            src_ref=prev_out.at[rows], dst_ref=inputs_fwd.at[rows],
            send_sem=pipe_send.at[0, h], recv_sem=pipe_recv.at[0, h],
            device_id={"pipe": lax.rem(section + 1, sections)}, device_id_type=MESH,
        )

    def relay_grad(h):
        cols = up_columns(h)
        return pltpu.make_async_remote_copy(
            src_ref=prev_grad.at[:, cols], dst_ref=all_up.at[own_rows, cols],
            send_sem=pipe_send.at[1, h], recv_sem=pipe_recv.at[1, h],
            device_id={"pipe": lax.rem(section + sections - 1, sections)}, device_id_type=MESH,
        )

    @pl.when(has_prev)
    def _():
        for h in range(2):
            relay_grad(h).start()

    @pl.when(has_next)
    def _():
        for h in range(2):
            relay_out(h).start()

    @pl.when(jnp.logical_not(has_prev))
    def _():
        load_fresh.start()

    @pl.when(jnp.logical_not(has_next))
    def _():
        load_cot.start()

    def block_of(ref):
        return lambda j: ref.at[pl.ds(pl.multiple_of(j * tokens, tokens), tokens)]

    def halves(ref, a):
        def view(h):
            return lambda j: ref.at[pl.ds(pl.multiple_of(j * tokens + h * half, half), half)]

        return [
            Gather(view(h), g_send.at[2 * a + h], g_recv.at[2 * a + h], chips, x, c)
            for h in range(2)
        ]

    def column_halves(ref, a, where):
        def view(h):
            cols = where(h)
            return lambda j: ref.at[pl.ds(pl.multiple_of(j * tokens, tokens), tokens), cols]

        return [
            Gather(view(h), g_send.at[2 * a + h], g_recv.at[2 * a + h], chips, x, c)
            for h in range(2)
        ]

    gather_bwd = halves(all_bwd, 0)
    gather_up = column_halves(all_up, 1, up_columns)
    gather_fwd = column_halves(all_fwd, 2, lambda h: pl.ds(h * (model // 2), model // 2))
    gather_gate = Gather(lambda j: gates_all.at[j], g_send.at[6], g_recv.at[6], chips, x, c)
    sems = [
        tuple(ref.at[a] for ref in (s_psend, s_precv, s_csend, s_crecv)) for a in range(2)
    ]
    scatter_row = Scatter(block_of(part), pair_row, cross_row, sems[0], chips, x, c)

    def narrow(j):
        return all_bwd.at[pl.ds(pl.multiple_of(j * tokens, tokens), tokens), pl.ds(0, model)]

    scatter_y = Scatter(narrow, pair_y, cross_y, sems[1], chips, x, c)

    def columns(k):
        return pl.ds(pl.multiple_of(k * chunk, chunk), chunk)

    every = model // chunk

    def chunks(body, begin=0, count=every):
        def step(k, carry):
            body(columns(begin + k))
            return carry

        lax.fori_loop(0, count, step, 0)

    lane = lax.broadcasted_iota(jnp.int32, (total, experts), 1).astype(jnp.float32)
    mine = (lane == me.astype(jnp.float32)).astype(jnp.float32)

    def project(rows_ref, at, ready):
        pre_acc[...] = jnp.zeros_like(pre_acc)
        log_acc[...] = jnp.zeros_like(log_acc)

        def body(cols):
            rows = rows_ref[:, cols]
            pre_acc[...] += dot(rows, gate_up_w[cols, :], 1, 0)
            log_acc[...] += dot(rows, router_b[:, cols], 1, 1)

        for h in range(2):
            ready(h)
            chunks(body, h * every // 2, every // 2)
        ids = all_bwd[:, model:].astype(jnp.float32)
        one = (lane == ids[:, at : at + 1]).astype(jnp.float32)
        two = (lane == ids[:, at + 1 : at + 2]).astype(jnp.float32)
        logits = log_acc[...]
        apart = jnp.sum((one - two) * logits, axis=1, keepdims=True)
        first, second = jax.nn.sigmoid(apart), jax.nn.sigmoid(-apart)
        weight = jnp.sum((one * first + two * second) * mine, axis=1, keepdims=True)
        return one, two, first, second, weight, pre_acc[:, :width], pre_acc[:, width:]

    gather_bwd[0].start()
    normalize_into(saved, all_bwd, 1)
    gather_bwd[1].start()

    @pl.when(jnp.logical_not(has_next))
    def _():
        load_cot.wait()

    for h in range(2):
        @pl.when(has_next)
        def _():
            relay_grad(h).wait_recv()

        gather_up[h].start()
        gather_bwd[h].forward()

    @pl.when(has_prev)
    def _():
        for h in range(2):
            relay_out(h).wait_recv()

    @pl.when(jnp.logical_not(has_prev))
    def _():
        load_fresh.wait()

    normalize_into(inputs_fwd, all_fwd, 0)
    normalize_into(inputs_fwd, all_fwd, 1)
    load_gate.wait()
    load_down.wait()
    for h in range(2):
        gather_bwd[h].finish()
    one, two, first, second, weight, gate, up = project(all_bwd, 0, lambda h: None)
    sig = jax.nn.sigmoid(gate)
    active = gate * sig
    hidden = active * up
    hid_weighted[...] = (weight * hidden).astype(jnp.bfloat16)

    def gu_copy(i, k):
        return pltpu.make_async_remote_copy(
            src_ref=gu_send.at[i - 1, k], dst_ref=gu_recv.at[i - 1, k],
            send_sem=gu_ss.at[i - 1, k], recv_sem=gu_rs.at[i - 1, k],
            device_id={"dp": lax.rem(dp + i, replicas)}, device_id_type=MESH,
        )

    def dn_copy(i, k):
        return pltpu.make_async_remote_copy(
            src_ref=dn_send.at[i - 1, k], dst_ref=dn_recv.at[i - 1, k],
            send_sem=dn_ss.at[i - 1, k], recv_sem=dn_rs.at[i - 1, k],
            device_id={"dp": lax.rem(dp + i, replicas)}, device_id_type=MESH,
        )

    def part_columns(owner, k):
        return pl.ds(pl.multiple_of(owner * piece + k * chunk, chunk), chunk)

    def gate_part(owner, k):
        cols = part_columns(owner, k)
        return dot(all_bwd[:, cols], grad_pre[...], 0, 0).astype(jnp.bfloat16)

    def down_part(owner, k):
        cols = part_columns(owner, k)
        return dot(hid_weighted[...], all_up[:, cols], 0, 0).astype(jnp.bfloat16)

    def send_down_parts():
        for i in range(1, replicas):
            def step(k, carry, i=i):
                dn_send[i - 1, k] = down_part(lax.rem(dp + i, replicas), k)
                dn_copy(i, k).start()
                return carry

            lax.fori_loop(0, steps, step, 0)

    gather_up[0].forward()
    hid_acc[...] = jnp.zeros_like(hid_acc)

    def up_body(cols):
        hid_acc[...] += dot(all_up[:, cols], down_w[:, cols], 1, 1)

    gather_up[0].finish()
    if replicas == 2:
        send_down_parts()
    chunks(up_body, up_half(0) * (every // 2), every // 2)
    gather_up[1].crossed()
    gather_fwd[0].start()
    gather_fwd[1].start()
    gather_up[1].pass_on()
    gather_up[1].finish()
    chunks(up_body, up_half(1) * (every // 2), every // 2)
    up_down = hid_acc[...]
    gate_grad = jnp.sum(hidden * up_down, axis=1, keepdims=True)
    lanes = lax.broadcasted_iota(jnp.int32, (total, 128), 1).astype(jnp.float32)
    gates_all[me] = (gate_grad * (lanes == me.astype(jnp.float32)).astype(jnp.float32)).astype(
        jnp.bfloat16
    )
    gather_gate.start()
    hidden_grad = weight * up_down
    grad_pre[:, :width] = (hidden_grad * up * sig * (1.0 + gate * (1.0 - sig))).astype(jnp.bfloat16)
    grad_pre[:, width:] = (hidden_grad * active).astype(jnp.bfloat16)

    for i in range(1, replicas):
        def send_step(k, carry, i=i):
            gu_send[i - 1, k] = gate_part(lax.rem(dp + i, replicas), k)
            gu_copy(i, k).start()
            return carry

        lax.fori_loop(0, steps, send_step, 0)
    if replicas != 2:
        send_down_parts()

    def row_body(cols):
        part[:, cols] = dot(grad_pre[...], gate_up_w[cols, :], 1, 1).astype(jnp.bfloat16)

    chunks(row_body)
    scatter_row.start()

    def own_step(k, carry):
        grad_gate_up[columns(k), :] = gate_part(dp, k)
        grad_down[:, columns(k)] = down_part(dp, k)
        return carry

    gather_gate.forward()
    scatter_row.forward()
    lax.fori_loop(0, steps, own_step, 0)

    gather_gate.finish()
    gate_all = gates_all[0].astype(jnp.float32)
    for j in range(1, owners):
        gate_all = gate_all + gates_all[j].astype(jnp.float32)
    logit = (one - two) * (
        first * second * jnp.sum((one - two) * gate_all[:, :experts], axis=1, keepdims=True)
    )
    logit_ref[...] = logit

    def rt_copy(i):
        return pltpu.make_async_remote_copy(
            src_ref=rt_send.at[i - 1], dst_ref=rt_recv.at[i - 1],
            send_sem=rt_ss.at[i - 1], recv_sem=rt_rs.at[i - 1],
            device_id={"dp": lax.rem(dp + i, replicas)}, device_id_type=MESH,
        )

    def router_part(owner):
        cols = pl.ds(pl.multiple_of(owner * piece + me * rt_step, 128), rt_width)
        return dot(
            logit_ref[...], all_bwd[:, cols].astype(jnp.float32), 0, 0, lax.Precision.HIGHEST
        )

    for i in range(1, replicas):
        rt_send[i - 1] = router_part(lax.rem(dp + i, replicas))
        rt_copy(i).start()
    rt_own[...] = router_part(dp)

    def fwd_ready(h):
        gather_fwd[h].forward()
        gather_fwd[h].finish()

    for h in range(2):
        gather_bwd[h].sent()
    _, _, _, _, weight_f, gate_f, up_f = project(all_fwd, 2, fwd_ready)
    hid_weighted[...] = (weight_f * (gate_f * jax.nn.sigmoid(gate_f) * up_f)).astype(jnp.bfloat16)

    def y_body(cols):
        all_bwd[:, cols] = dot(hid_weighted[...], down_w[:, cols], 1, 0).astype(jnp.bfloat16)

    chunks(y_body)
    scatter_y.start()
    scatter_y.forward()

    scatter_row.finish()

    def grad_body(at):
        rows = pl.ds(at, STRIP)
        home = pl.ds(pl.multiple_of(me * tokens + at, STRIP), STRIP)
        values = saved[rows, :].astype(jnp.float32)
        inv = inverse(values)
        unit = values * inv
        normed_grad = scatter_row.total(rows)
        steps_here = logit_ref[home, :]
        for j in range(experts):
            normed_grad = normed_grad + steps_here[:, j : j + 1] * router_b[j : j + 1, :].astype(
                jnp.float32
            )
        inner = jnp.mean(normed_grad * unit, axis=1, keepdims=True)
        input_grad[rows, :] = (
            all_up[home, :].astype(jnp.float32) + (normed_grad - unit * inner) * inv
        ).astype(jnp.bfloat16)

    strips(grad_body)

    rt = rt_own[...]
    for i in range(1, replicas):
        rt_copy(i).wait_recv()
        rt = rt + rt_recv[i - 1]
    grad_router[...] = rt

    for i in range(1, replicas):
        def add_step(k, carry, i=i):
            gu_copy(i, k).wait_recv()
            dn_copy(i, k).wait_recv()
            cols = columns(k)
            grad_gate_up[cols, :] = (
                grad_gate_up[cols, :].astype(jnp.float32) + gu_recv[i - 1, k].astype(jnp.float32)
            ).astype(jnp.bfloat16)
            grad_down[:, cols] = (
                grad_down[:, cols].astype(jnp.float32) + dn_recv[i - 1, k].astype(jnp.float32)
            ).astype(jnp.bfloat16)
            return carry

        lax.fori_loop(0, steps, add_step, 0)

    scatter_y.finish()

    def out_body(at):
        rows = pl.ds(at, STRIP)
        section_out[rows, :] = (
            inputs_fwd[rows, :].astype(jnp.float32) + scatter_y.total(rows)
        ).astype(jnp.bfloat16)

    strips(out_body)

    @pl.when(has_prev)
    def _():
        for h in range(2):
            relay_grad(h).wait_send()

    @pl.when(has_next)
    def _():
        for h in range(2):
            relay_out(h).wait_send()

    for h in range(2):
        gather_up[h].sent()
        gather_fwd[h].sent()
    gather_gate.sent()
    scatter_row.sent()
    scatter_y.sent()
    for i in range(1, replicas):
        rt_copy(i).wait_send()

        def drain(k, carry, i=i):
            gu_copy(i, k).wait_send()
            dn_copy(i, k).wait_send()
            return carry

        lax.fori_loop(0, steps, drain, 0)


def hand_over(*refs):
    sources, targets, stages, arrive, leave = refs[:5], refs[5:10], refs[10:15], refs[15], refs[16]
    copies = []
    for a in range(5):
        rows = sources[a].shape[0]
        parts = 2 if rows % 32 == 0 else 1
        for h in range(parts):
            at = pl.ds(h * (rows // parts), rows // parts)
            copies.append(
                (
                    pltpu.make_async_copy(sources[a].at[at], stages[a].at[at], arrive.at[a, h]),
                    pltpu.make_async_copy(stages[a].at[at], targets[a].at[at], leave.at[a, h]),
                )
            )
    for first, _ in copies:
        first.start()
    for first, then in copies:
        first.wait()
        then.start()
    for _, then in copies:
        then.wait()


def shards(
    fresh, cotangent, prev_out, prev_grad, saved_in, route_fwd, route_bwd, router, gate_up, down
):
    sections = lax.axis_size("pipe")
    replicas = lax.axis_size("dp")
    owners = lax.axis_size("expert")
    tokens, model = fresh.shape
    width = down.shape[2]
    experts = router.shape[2]
    chips = owners // 2
    total = owners * tokens
    piece = model // replicas
    chunk = min(768, piece)
    steps = piece // chunk
    rt_width = piece // owners if (piece // owners) % 128 == 0 else piece

    bf16, f32 = jnp.bfloat16, jnp.float32
    far = max(replicas - 1, 1)
    dma = pltpu.SemaphoreType.DMA
    hbm = pl.BlockSpec(memory_space=pltpu.HBM)
    vmem = pl.BlockSpec(memory_space=pltpu.VMEM)
    outs = pl.pallas_call(
        functools.partial(kernel, (sections, replicas, owners)),
        out_shape=(
            jax.ShapeDtypeStruct((tokens, model), bf16),
            jax.ShapeDtypeStruct((tokens, model), bf16),
            jax.ShapeDtypeStruct((piece, 2 * width), bf16),
            jax.ShapeDtypeStruct((width, piece), bf16),
            jax.ShapeDtypeStruct((experts, rt_width), f32),
        ),
        in_specs=[hbm] * 5 + [vmem] * 3 + [hbm] * 2,
        out_specs=(vmem,) * 5,
        scratch_shapes=[
            pltpu.VMEM((total, model + 128), bf16),
            pltpu.VMEM((total, model), bf16),
            pltpu.VMEM((total, model), bf16),
            pltpu.VMEM((total, model), bf16),
            pltpu.VMEM((chips, tokens, model), bf16),
            pltpu.VMEM((chips - 1, tokens, model), bf16),
            pltpu.VMEM((chips, tokens, model), bf16),
            pltpu.VMEM((chips - 1, tokens, model), bf16),
            pltpu.VMEM((model, 2 * width), bf16),
            pltpu.VMEM((width, model), bf16),
            pltpu.VMEM((tokens, model), bf16),
            pltpu.VMEM((tokens, model), bf16),
            pltpu.VMEM((far, steps, chunk, 2 * width), bf16),
            pltpu.VMEM((far, steps, chunk, 2 * width), bf16),
            pltpu.VMEM((far, steps, width, chunk), bf16),
            pltpu.VMEM((far, steps, width, chunk), bf16),
            pltpu.VMEM((far, experts, rt_width), f32),
            pltpu.VMEM((far, experts, rt_width), f32),
            pltpu.VMEM((owners, total, 128), bf16),
            pltpu.VMEM((total, 2 * width), f32),
            pltpu.VMEM((total, experts), f32),
            pltpu.VMEM((total, width), f32),
            pltpu.VMEM((total, 2 * width), bf16),
            pltpu.VMEM((total, width), bf16),
            pltpu.VMEM((total, experts), f32),
            pltpu.VMEM((experts, rt_width), f32),
            dma((5,)),
            dma((2, 2)),
            dma((2, 2)),
            dma((7, 2 * chips - 1)),
            dma((7, 2 * chips - 1)),
            dma((2, chips)),
            dma((2, chips)),
            dma((2, chips - 1)),
            dma((2, chips - 1)),
            dma((far, steps)),
            dma((far, steps)),
            dma((far, steps)),
            dma((far, steps)),
            dma((far,)),
            dma((far,)),
        ],
        compiler_params=pltpu.CompilerParams(
            collective_id=0, has_side_effects=True, vmem_limit_bytes=60 * 2**20
        ),
        name="relay_step",
    )(
        fresh, cotangent, prev_out[0], prev_grad[0], saved_in[0],
        route_bwd[0].T, route_fwd[0].T, router[0].T, gate_up[0, 0], down[0, 0],
    )
    section_out, input_grad, grad_gate_up, grad_down, grad_router = pl.pallas_call(
        hand_over,
        out_shape=[jax.ShapeDtypeStruct(out.shape, out.dtype) for out in outs],
        in_specs=[hbm] * 5,
        out_specs=[hbm] * 5,
        scratch_shapes=[pltpu.VMEM(out.shape, out.dtype) for out in outs]
        + [dma((5, 2)), dma((5, 2))],
        compiler_params=pltpu.CompilerParams(vmem_limit_bytes=60 * 2**20),
        name="hand_over",
    )(*outs)
    share = piece // owners
    if rt_width != share:
        grad_router = lax.dynamic_slice_in_dim(
            grad_router, lax.axis_index("expert") * share, share, axis=1
        )
    return (
        section_out[None],
        input_grad[None],
        grad_gate_up[None, None],
        grad_down[None, None],
        grad_router.T[None],
    )


def solution(mesh):
    tokens = P(("dp", "expert"), None)
    sectioned = P("pipe", ("dp", "expert"), None)
    return jax.shard_map(
        shards,
        mesh=mesh,
        in_specs=(
            tokens, tokens, sectioned, sectioned, sectioned, sectioned, sectioned,
            P("pipe", None, None),
            P("pipe", "expert", None, None),
            P("pipe", "expert", None, None),
        ),
        out_specs=(
            sectioned,
            sectioned,
            P("pipe", "expert", "dp", None),
            P("pipe", "expert", None, "dp"),
            sectioned,
        ),
        check_vma=False,
    )
```
